32 devices in a mesh: group: 2 (over y), gx: 4 (over z), gy: 2 (over x), gz: 2 (over core).
Axes of the slice: x: 2, y: 2, z: 4, core: 2. Of those that a mesh axis runs over, the one named last changes fastest.
Arguments:
- tokens: bfloat16 [12, 8192], P('group', 'gx'), parts along dimension 0, may hold values from -40 to 40
- norm_gain: float32 [8192], P('gx'), may hold values from 0.1 to 1.9
- q_weight: bfloat16 [8192, 4096], P('gx', ('gy', 'gz')), may hold values from -0.0625 to 0.0625
- kv_weight: bfloat16 [8192, 512], P('gx'), may hold values from -0.0625 to 0.0625
- out_weight: bfloat16 [4096, 8192], P(('gy', 'gz'), 'gx'), may hold values from -0.09375 to 0.09375
- gate_weight: bfloat16 [8192, 16384], P('gx', ('gy', 'gz')), may hold values from -0.0625 to 0.0625
- up_weight: bfloat16 [8192, 16384], P('gx', ('gy', 'gz')), may hold values from -0.0625 to 0.0625
- down_weight: bfloat16 [16384, 8192], P(('gy', 'gz'), 'gx'), may hold values from -0.046875 to 0.046875
- kv_cache: bfloat16 [12, 2048, 512], P(('group', 'gy'), ('gx', 'gz')), parts along dimension 0, may hold values from -55 to 55
- lengths: int32 [12], P(('group', 'gy')), parts along dimension 0, may hold values from 1026 to 2048, as said below
Outputs:
- mixed: bfloat16 [12, 8192], P('group', 'gx'), parts along dimension 0
- new_kv: bfloat16 [12, 512], P(('group', 'gy')), parts along dimension 0
The draws below stay inside these ranges and needn't reach their ends.
There are 2 independent parts, one for each index of `group`. The reference program is written for one: setup_inputs(seed, part) draws one part's arguments, and reference() takes and returns one part's arrays. A program takes and returns all parts, laid end to end along the dimension named above; an argument that names none is the same for every part. Nothing has to cross between parts.
Inputs may be any that keep to these rules, and one draw needn't show every extreme that they name: The new token of sequence s stands at position lengths[s]; cache positions from lengths[s] on hold no valid token; some sequence has all 2048 positions valid.
All inputs are finite; a program needn't handle non-finite values.
Results may differ from the reference program's by a relative error of at most 0.012.
Values may be sent and summed in bfloat16 or wider, within the bound.
No kernel may reach another device: no remote copies, remote signals or barrier semaphores. Data moves between devices by JAX's collectives and lax.ppermute only.
A program may use at most 128 MiB of HBM per device.

```python
import jax
import jax.numpy as jnp
from jax import lax

D = 8192
FF = 16384
HEADS = 16
HEAD_DIM = 256
SEQS = 6
CTX = 2048


def draw_tokens(key, part):
    first_key, second_key = jax.random.split(jax.random.fold_in(key, 11), 2)
    place = jnp.arange(D, dtype=jnp.float32) / D
    rough = jax.random.uniform(second_key, (D,), jnp.float32, 0.5, 1.5)
    noise = jax.random.normal(first_key, (SEQS, D), jnp.float32)
    col_scales = 3.0 ** (place - 0.5) * rough
    values = jnp.clip(noise, -4.0, 4.0) * col_scales[None, :]
    return jnp.clip(values, -40.0, 40.0).astype(jnp.bfloat16)


def draw_lengths(key, part):
    first_key, second_key = jax.random.split(jax.random.fold_in(key, 37), 2)
    drawn = jax.random.randint(first_key, (SEQS,), CTX // 2 + 2, CTX + 1)
    full_row = jax.random.randint(second_key, (), 0, SEQS)
    rows = jnp.arange(SEQS, dtype=jnp.int32)
    return jnp.where(rows == full_row, CTX, drawn).astype(jnp.int32)


def draw_kv_cache(key, part):
    first_key = jax.random.fold_in(jax.random.fold_in(key, 23), 0)
    second_key = jax.random.fold_in(jax.random.fold_in(key, 23), 1)
    fourth_key = jax.random.fold_in(jax.random.fold_in(key, 23), 3)
    fifth_key = jax.random.fold_in(jax.random.fold_in(key, 23), 4)
    keys = 2.5 * jnp.clip(jax.random.normal(first_key, (SEQS, CTX, HEAD_DIM), jnp.float32), -4.0, 4.0)
    values = 1.5 * jnp.clip(jax.random.normal(second_key, (SEQS, CTX, HEAD_DIM), jnp.float32), -4.0, 4.0)
    strength = jax.random.uniform(fourth_key, (SEQS, 1, 1), jnp.float32, 30.0, 45.0)
    signs = jax.random.randint(fifth_key, (SEQS, 1, HEAD_DIM), 0, 2).astype(jnp.float32) * 2.0 - 1.0
    factors = jnp.array([1.0, 1.02], jnp.float32)[None, :, None]
    strong = strength * signs * factors
    half = CTX // 2
    keys = jnp.concatenate([keys[:, :half, :], strong, keys[:, half + 2:, :]], 1)
    return jnp.concatenate([keys, values], 2).astype(jnp.bfloat16)


def block_levels(key, dims, cuts, low, largest):
    level = 1.0
    for position, shards_of in cuts:
        heights = jax.random.uniform(jax.random.fold_in(jax.random.fold_in(key, 6), position), (shards_of,), jnp.float32, low / len(cuts), largest / len(cuts))
        level = level * jnp.repeat(jnp.exp(heights), dims[position] // shards_of).reshape((-1,) + (1,) * (len(dims) - 1 - position))
    return level


def centred(key, extent, scale, most, pieces=(), held_as=jnp.bfloat16):
    values = scale * jax.random.normal(key, extent, jnp.float32)
    if pieces:
        values = values * block_levels(key, extent, pieces, -0.22, 0.18)
    return jnp.clip(values, -most, most).astype(held_as)


def setup_inputs(seed: int = 0, part: int = 0) -> dict:
    streams_of = jax.random.split(jax.random.key(seed), 11)
    part_keys = jax.random.split(jax.random.fold_in(streams_of[10], part), 11)
    tokens = draw_tokens(jax.random.fold_in(jax.random.fold_in(streams_of[10], part), 71), part)
    norm_gain = jnp.clip(1.0 + 0.18 * jax.random.normal(streams_of[1], (D,), jnp.float32), 0.1, 1.9)
    q_weight = centred(streams_of[2], (D, HEADS * HEAD_DIM), D ** -0.5, 0.0625, ((0, 4), (1, 4)))
    kv_weight = centred(streams_of[3], (D, 2 * HEAD_DIM), D ** -0.5, 0.0625, ((0, 4),))
    out_weight = centred(streams_of[4], (HEADS * HEAD_DIM, D), (HEADS * HEAD_DIM) ** -0.5, 0.09375, ((0, 4), (1, 4)))
    gate_weight = centred(streams_of[5], (D, FF), D ** -0.5, 0.0625, ((0, 4), (1, 4)))
    up_weight = centred(streams_of[6], (D, FF), D ** -0.5, 0.0625, ((0, 4), (1, 4)))
    down_weight = centred(streams_of[7], (FF, D), FF ** -0.5, 0.046875, ((0, 4), (1, 4)))
    kv_cache = draw_kv_cache(jax.random.fold_in(jax.random.fold_in(streams_of[10], part), 71), part)
    lengths = draw_lengths(jax.random.fold_in(jax.random.fold_in(streams_of[10], part), 71), part)
    return {"tokens": tokens, "norm_gain": norm_gain, "q_weight": q_weight, "kv_weight": kv_weight, "out_weight": out_weight, "gate_weight": gate_weight, "up_weight": up_weight, "down_weight": down_weight, "kv_cache": kv_cache, "lengths": lengths}


epsilon = 1e-05
masked_fill = -1e+30
rotary_base = 10000.0

def rotate(values, angle):
    middle = values.shape[-1] // 2
    first = values[..., :middle]
    second = values[..., middle:]
    cosine = jnp.cos(angle)
    sine_part = jnp.sin(angle)
    return jnp.concatenate([first * cosine - second * sine_part, first * sine_part + second * cosine], -1)

def angles(lengths, head_dim):
    middle = head_dim // 2
    spread = rotary_base ** (-jnp.arange(middle, dtype=jnp.float32) / middle)
    return lengths.astype(jnp.float32)[:, None] * spread[None, :]

def reference(tokens, norm_gain, q_weight, kv_weight, out_weight, gate_weight, up_weight, down_weight, kv_cache, lengths):
    inputs = tokens.astype(jnp.float32)
    center = lax.optimization_barrier(jnp.sum(inputs, 1)) / D
    spread_sq = lax.optimization_barrier(jnp.sum(inputs * inputs, 1)) / D - center * center
    normed = ((inputs - center[:, None]) * lax.rsqrt(spread_sq + epsilon)[:, None] * norm_gain[None, :]).astype(jnp.bfloat16)
    query = jnp.dot(normed, q_weight, preferred_element_type=jnp.float32).astype(jnp.bfloat16)
    keyval = jnp.dot(normed, kv_weight, preferred_element_type=jnp.float32)
    gate = jnp.dot(normed, gate_weight, preferred_element_type=jnp.float32)
    upward = jnp.dot(normed, up_weight, preferred_element_type=jnp.float32)
    hidden = (jax.nn.silu(gate) * upward).astype(jnp.bfloat16)
    angle = angles(lengths, HEAD_DIM)
    new_kv = jnp.concatenate([rotate(keyval[:, :HEAD_DIM], angle), keyval[:, HEAD_DIM:]], 1).astype(jnp.bfloat16)
    rotated = rotate(query.astype(jnp.float32).reshape(SEQS, HEADS, HEAD_DIM), angle[:, None, :]).astype(jnp.bfloat16)
    scale = HEAD_DIM ** (-0.5)
    positions = jnp.arange(CTX, dtype=jnp.int32)

    def one_sequence(packed):
        queries, cache, length, key_new, value_new = packed
        scores = jnp.dot(queries, cache[:, :HEAD_DIM].T, preferred_element_type=jnp.float32) * scale
        own_score = jnp.dot(queries, key_new, preferred_element_type=jnp.float32) * scale
        live = positions < length
        hidden_scores = jnp.where(live[None, :], scores, masked_fill)
        top = jnp.maximum(lax.optimization_barrier(jnp.max(hidden_scores, 1)), own_score)
        weights = jnp.where(live[None, :], jnp.exp(hidden_scores - top[:, None]), 0.0)
        numer = jnp.dot(weights.astype(jnp.bfloat16), cache[:, HEAD_DIM:], preferred_element_type=jnp.float32)
        denom = lax.optimization_barrier(jnp.sum(weights, 1))
        own_weight = jnp.exp(own_score - top)
        numer = numer + own_weight[:, None] * value_new.astype(jnp.float32)[None, :]
        denom = denom + own_weight
        return (numer / denom[:, None]).astype(jnp.bfloat16)
    attended = lax.map(one_sequence, (rotated, kv_cache, lengths, new_kv[:, :HEAD_DIM], new_kv[:, HEAD_DIM:]))
    attended = attended.reshape(SEQS, HEADS * HEAD_DIM)
    total = jnp.dot(attended, out_weight, preferred_element_type=jnp.float32) + jnp.dot(hidden, down_weight, preferred_element_type=jnp.float32)
    mixed = (inputs + total).astype(jnp.bfloat16)
    return (mixed, new_kv)
```

```python
import jax
import jax.numpy as jnp
from jax import lax
from jax.sharding import PartitionSpec as P

epsilon = 1e-05
masked_fill = -1e30
rotary_base = 10000.0
PART = ("gx", "gy", "gz")
FEW = 8


def rotate(values, angle):
    middle = values.shape[-1] // 2
    first = values[..., :middle]
    second = values[..., middle:]
    cosine = jnp.cos(angle)
    sine_part = jnp.sin(angle)
    return jnp.concatenate(
        [first * cosine - second * sine_part, first * sine_part + second * cosine], -1
    )


def angles(lengths, head_dim):
    middle = head_dim // 2
    spread = rotary_base ** (-jnp.arange(middle, dtype=jnp.float32) / middle)
    return lengths.astype(jnp.float32)[:, None] * spread[None, :]


def in_thirds(values):
    high = lax.reduce_precision(values, 8, 7)
    rest = values - high
    middle = lax.reduce_precision(rest, 8, 7)
    return jnp.stack([high, middle, rest - middle], -1).astype(jnp.bfloat16)


def from_thirds(terms):
    terms = terms.astype(jnp.float32)
    return terms[..., 0] + (terms[..., 1] + terms[..., 2])


def from_others(values, axis):
    size = lax.axis_size(axis)
    return [
        lax.ppermute(values, axis, [(place, place ^ step) for place in range(size)])
        for step in range(1, size)
    ]


def body(
    tokens,
    norm_gain,
    q_weight,
    kv_weight,
    out_weight,
    gate_weight,
    up_weight,
    down_weight,
    kv_cache,
    lengths,
):
    gx, gy, gz = (lax.axis_size(axis) for axis in PART)
    cols = gy * gz
    seqs, width = tokens.shape
    seq_dev = lengths.shape[0]
    head_dim = kv_weight.shape[1] // 2
    q_dev = q_weight.shape[1]
    heads_dev = q_dev // head_dim
    heads = heads_dev * cols
    kv_dev = kv_weight.shape[1] // cols
    ctx_dev = kv_cache.shape[1]
    row = lax.axis_index("gy")
    col = lax.axis_index(("gy", "gz"))

    inputs = tokens.astype(jnp.float32)
    mean_dev = jnp.sum(inputs, 1) / width
    centred = inputs - mean_dev[:, None]
    square_dev = jnp.sum(centred * centred, 1)
    lhs = jnp.concatenate([centred * norm_gain[None, :], norm_gain[None, :]], 0).astype(jnp.bfloat16)

    def project(weight):
        return jnp.dot(lhs, weight, preferred_element_type=jnp.float32)

    kv_own = lax.dynamic_slice_in_dim(kv_weight, col * kv_dev, kv_dev, 1)
    first = jnp.concatenate([project(q_weight), project(kv_own)], 1).astype(jnp.bfloat16)
    stats = in_thirds(jnp.stack([mean_dev, square_dev])).reshape(-1)
    extra = -(-stats.shape[0] // 128) * 128
    stats = jnp.pad(stats, (0, extra - stats.shape[0]))
    by_row = first[:seqs].reshape(gy, seq_dev, -1)
    gain_row = jnp.broadcast_to(first[seqs], (gy, 1, first.shape[1]))
    by_row = jnp.concatenate([by_row, gain_row], 1)
    by_row = jnp.concatenate(
        [by_row, jnp.broadcast_to(stats, (gy, seq_dev + 1, extra))], 2
    )
    sent = jnp.broadcast_to(by_row[None, :, None], (gx, gy, gz) + by_row.shape[1:])
    sent = sent.reshape((gx * cols,) + by_row.shape[1:])
    got = lax.all_to_all(sent, PART, split_axis=0, concat_axis=0, tiled=True)
    got = got.reshape((gx, cols) + by_row.shape[1:])

    gate_part = project(gate_weight).astype(jnp.bfloat16)
    up_part = project(up_weight).astype(jnp.bfloat16)

    stats = from_thirds(got[:, 0, 0, -extra:][:, : seqs * 6].reshape(gx, 2, seqs, 3))
    means = stats[:, 0]
    center = jnp.sum(means, 0) / gx
    shift = means - center
    spread_sq = jnp.sum(stats[:, 1], 0) / (width * gx) + jnp.sum(shift * shift, 0) / gx
    inverse = lax.rsqrt(spread_sq + epsilon)

    def whole(parts, shift, inverse):
        total = 0.0
        for source in range(gx):
            part = parts[source].astype(jnp.float32)
            total += part[..., :-1, :] + shift[source][:, None] * part[..., -1:, :]
        return total * inverse[:, None]

    shift_row = lax.dynamic_slice_in_dim(shift, row * seq_dev, seq_dev, 1)
    inverse_row = lax.dynamic_slice_in_dim(inverse, row * seq_dev, seq_dev, 0)
    summed = whole([got[s, :, :, : q_dev + kv_dev] for s in range(gx)], shift_row, inverse_row)
    query = summed[..., :q_dev].astype(jnp.bfloat16)
    keyval = summed[..., q_dev:].transpose(1, 0, 2).reshape(seq_dev, -1)
    angle = angles(lengths, head_dim)
    new_kv = jnp.concatenate(
        [rotate(keyval[:, :head_dim], angle), keyval[:, head_dim:]], 1
    ).astype(jnp.bfloat16)
    query = query.reshape(cols, seq_dev, heads_dev, head_dim).transpose(1, 0, 2, 3)
    query = query.reshape(seq_dev, heads, head_dim)
    rotated = rotate(query.astype(jnp.float32), angle[:, None, :]).astype(jnp.bfloat16)

    block = lax.axis_index(("gx", "gz"))
    positions = block * ctx_dev + jnp.arange(ctx_dev, dtype=jnp.int32)
    live = positions[None, :] < lengths[:, None]
    scale = head_dim ** (-0.5)
    scores = (
        jnp.einsum(
            "shd,scd->shc", rotated, kv_cache[:, :, :head_dim], preferred_element_type=jnp.float32
        )
        * scale
    )
    own_score = (
        jnp.sum(rotated.astype(jnp.float32) * new_kv[:, None, :head_dim].astype(jnp.float32), -1)
        * scale
    )
    masked = jnp.where(live[:, None, :], scores, masked_fill)
    top = jnp.maximum(jnp.max(masked, 2), own_score)
    weights = jnp.where(live[:, None, :], jnp.exp(masked - top[..., None]), 0.0)
    own_weight = jnp.where(block == 0, jnp.exp(own_score - top), 0.0)
    numer = jnp.einsum(
        "shc,scd->shd",
        weights.astype(jnp.bfloat16),
        kv_cache[:, :, head_dim:],
        preferred_element_type=jnp.float32,
    )
    numer = numer + own_weight[..., None] * new_kv[:, None, head_dim:].astype(jnp.float32)
    denom = jnp.sum(weights, 2) + own_weight

    marks = in_thirds(jnp.stack([top, denom], -1)).reshape(seq_dev, heads, 6)
    marks = jnp.pad(marks, ((0, 0), (0, 0), (0, 122)))
    partial = jnp.concatenate([numer.astype(jnp.bfloat16), marks], 2)
    partial = partial.reshape(seq_dev, cols, heads_dev, -1).transpose(1, 0, 2, 3)
    sent = jnp.broadcast_to(partial[None], (gx,) + partial.shape)
    sent = sent.reshape(gx * cols, seq_dev * heads_dev, -1)
    got = lax.all_to_all(sent, PART, split_axis=0, concat_axis=0, tiled=True)

    both = jnp.concatenate([gate_part, up_part], 1)
    parts = [both] + from_others(both, "gx")
    place = lax.axis_index("gx")
    shifts = [
        lax.dynamic_index_in_dim(shift, place ^ step, 0, False) for step in range(gx)
    ]
    summed = whole(parts, shifts, inverse)
    ff_dev = gate_weight.shape[1]
    hidden = (jax.nn.silu(summed[:, :ff_dev]) * summed[:, ff_dev:]).astype(jnp.bfloat16)
    total = jnp.dot(hidden, down_weight, preferred_element_type=jnp.float32)

    got = got.reshape(gx, gy, gz, seq_dev, heads_dev, -1)
    marks = from_thirds(got[..., head_dim : head_dim + 6].reshape(got.shape[:-1] + (2, 3)))
    tops, denoms = marks[..., 0], marks[..., 1]
    factor = jnp.exp(tops - jnp.max(tops, (0, 2), keepdims=True))
    denom = jnp.sum(denoms * factor, (0, 2))
    numer = jnp.sum(got[..., :head_dim].astype(jnp.float32) * factor[..., None], (0, 2))
    attended = (numer / denom[..., None]).astype(jnp.bfloat16).reshape(seqs, q_dev)
    total = total + jnp.dot(attended, out_weight, preferred_element_type=jnp.float32)

    share = total.astype(jnp.bfloat16)
    for other in from_others(share, ("gy", "gz")):
        total = total + other.astype(jnp.float32)
    mixed = (inputs + total).astype(jnp.bfloat16)
    return (mixed, new_kv)


def solution(mesh):
    in_specs = (
        P("group", "gx"),
        P("gx"),
        P("gx", ("gy", "gz")),
        P("gx", None),
        P(("gy", "gz"), "gx"),
        P("gx", ("gy", "gz")),
        P("gx", ("gy", "gz")),
        P(("gy", "gz"), "gx"),
        P(("group", "gy"), ("gx", "gz"), None),
        P(("group", "gy")),
    )
    out_specs = (P("group", "gx"), P(("group", "gy"), None))
    return jax.shard_map(body, mesh=mesh, in_specs=in_specs, out_specs=out_specs, check_vma=False)
```

```python
import functools

import jax
import jax.numpy as jnp
from jax import lax
from jax.experimental import pallas as pl
from jax.experimental.pallas import tpu as pltpu
from jax.sharding import PartitionSpec as P

epsilon = 1e-05
masked_fill = -1e30
rotary_base = 10000.0
PART = ("gx", "gy", "gz")
FEW = 8
F32 = jnp.float32
BF16 = jnp.bfloat16
VMEM = pl.BlockSpec(memory_space=pltpu.VMEM)
SMEM = pl.BlockSpec(memory_space=pltpu.SMEM)
ANY = pl.BlockSpec(memory_space=pl.ANY)


def angles(lengths, head_dim):
    middle = head_dim // 2
    spread = rotary_base ** (-jnp.arange(middle, dtype=F32) / middle)
    return lengths.astype(F32)[:, None] * spread[None, :]


def iota(shape, dim):
    return lax.broadcasted_iota(jnp.int32, shape, dim)


def thirds(values):
    high = values.astype(BF16).astype(F32)
    rest = values - high
    middle = rest.astype(BF16).astype(F32)
    return high, middle, rest - middle


def from_lanes(row, first, count):
    lane = iota(row.shape, 1)
    return jnp.sum(jnp.where((lane >= first) & (lane < first + count), row, 0.0), 1, keepdims=True)


def rotated_halves(values, cosine, sine):
    middle = values.shape[-1] // 2
    first, second = values[:, :middle], values[:, middle:]
    return jnp.concatenate(
        [first * cosine - second * sine, first * sine + second * cosine], 1
    )


def cost(flops, nbytes):
    return pl.CostEstimate(flops=flops, bytes_accessed=nbytes, transcendentals=0)


def params():
    return pltpu.CompilerParams(vmem_limit_bytes=24 * 2**20)


def first_kernel(dims, tokens, gain, q_hbm, kv_hbm, sent, lhs, rows, wq, wkv, q_sem, kv_sem):
    gx, gy, gz, seq_dev, pieces = dims
    depth = q_hbm.shape[0] // pieces
    kv_dev = wkv.shape[1]
    cols = gy * gz
    col = lax.axis_index("gy") * gz + lax.axis_index("gz")
    kv_own = kv_hbm
    if kv_hbm.shape[1] != kv_dev:
        kv_own = kv_hbm.at[:, pl.ds(pl.multiple_of(col * kv_dev, kv_dev), kv_dev)]
    kv_copy = pltpu.make_async_copy(kv_own, wkv, kv_sem)
    q_copies = []
    for piece in range(pieces):
        part = pl.ds(piece * depth, depth)
        copy = pltpu.make_async_copy(q_hbm.at[part], wq.at[part], q_sem.at[piece])
        copy.start()
        q_copies.append(copy)
    kv_copy.start()

    inputs = tokens[...].astype(F32)
    seqs, width = inputs.shape
    mean = jnp.sum(inputs, 1, keepdims=True) / width
    centred = inputs - mean
    square = jnp.sum(centred * centred, 1, keepdims=True)
    scaled = centred * gain[...]
    each = seq_dev + 1
    for a in range(gy):
        rows[a * each : a * each + seq_dev, :] = scaled[a * seq_dev : (a + 1) * seq_dev]
        rows[a * each + seq_dev : (a + 1) * each, :] = gain[...]
    lhs[...] = rows[...].astype(BF16)

    lanes = sent.shape[2] - wq.shape[1] - kv_dev
    lane = iota((seqs, lanes), 1)
    first = iota((seqs, lanes), 0) * 6
    marks = jnp.zeros((seqs, lanes), F32)
    for place, term in enumerate(thirds(mean) + thirds(square)):
        marks = jnp.where(lane == first + place, term, marks)
    marks = jnp.broadcast_to(jnp.sum(marks, 0, keepdims=True), (each, lanes))

    total = jnp.zeros((gy * each, wq.shape[1]), F32)
    for piece in range(pieces):
        part = slice(piece * depth, (piece + 1) * depth)
        q_copies[piece].wait()
        total += jnp.dot(lhs[:, part], wq[part, :], preferred_element_type=F32)
    kv_copy.wait()
    keyval = jnp.dot(lhs[...], wkv[...], preferred_element_type=F32)
    whole = jnp.concatenate([total, keyval], 1)
    for a in range(gy):
        piece = jnp.concatenate([whole[a * each : (a + 1) * each], marks], 1).astype(BF16)
        for i in range(gx):
            for b in range(gz):
                sent[(i * gy + a) * gz + b] = piece


def attention_kernel(dims, got, cache, lengths, tables, sent, new_kv, stats, qs, ks, vs):
    gx, gy, gz, seq_dev, q_dev, kv_dev, features = dims
    cols = gy * gz
    each = seq_dev + 1
    ctx_dev = cache.shape[1]
    head_dim = cache.shape[2] // 2
    heads_dev = q_dev // head_dim
    heads = heads_dev * cols
    width = q_dev + kv_dev
    row = lax.axis_index("gy")
    block = lax.axis_index("gx") * gz + lax.axis_index("gz")

    marks = [got[i * cols][:, width:].astype(F32)[:1] for i in range(gx)]
    lanes = marks[0].shape[1]

    def centre(count, sequence, valid):
        first = sequence * 6
        means, squares = [], 0.0
        for i in range(gx):
            mine = jnp.broadcast_to(marks[i], (count, lanes))
            means.append(jnp.where(valid, from_lanes(mine, first, 3), 0.0))
            squares += from_lanes(mine, first + 3, 3)
        center = sum(means) / gx
        shifts = [mean - center for mean in means]
        spread = squares / features + sum(s * s for s in shifts) / gx
        return shifts, jnp.where(valid, lax.rsqrt(spread + epsilon), 0.0)

    rows = gy * each
    place = iota((rows, 1), 0)
    shifts, inverse = centre(rows, place // each * seq_dev + place % each, place % each < seq_dev)
    for i in range(gx):
        stats[i] = jnp.broadcast_to(shifts[i], stats.shape[1:])
    stats[gx] = jnp.broadcast_to(inverse, stats.shape[1:])

    place = iota((each, 1), 0)
    shifts, inverse = centre(each, row * seq_dev + place, place < seq_dev)

    cosine, sine = tables[0], tables[1]
    keyval = []
    for c in range(cols):
        total = 0.0
        for i in range(gx):
            part = got[i * cols + c][:, :width].astype(F32)
            total += part + shifts[i] * part[seq_dev:]
        total = total * inverse
        keyval.append(total[:, q_dev:])
        query = total[:, :q_dev].astype(BF16).astype(F32)
        for h in range(heads_dev):
            turned = rotated_halves(query[:, h * head_dim : (h + 1) * head_dim], cosine, sine)
            head = c * heads_dev + h
            qs[head * each : (head + 1) * each, :] = turned
    keyval = jnp.concatenate(keyval, 1)
    fresh = jnp.concatenate(
        [rotated_halves(keyval[:, :head_dim], cosine, sine), keyval[:, head_dim:]], 1
    ).astype(BF16)
    new_kv[...] = fresh[:seq_dev]
    fresh = fresh.astype(F32)
    for head in range(heads):
        ks[head * each : (head + 1) * each, :] = fresh[:, :head_dim]
        vs[head * each : (head + 1) * each, :] = fresh[:, head_dim:]

    many = heads * each
    scale = head_dim ** (-0.5)
    queries = qs[...].astype(BF16)
    own = jnp.sum(queries.astype(F32) * ks[...], 1, keepdims=True) * scale
    place = iota((many, 1), 0) % each
    position = block * ctx_dev + iota((many, ctx_dev), 1)
    scores = jnp.full((many, ctx_dev), masked_fill, F32)
    for s in range(seq_dev):
        found = lax.dot_general(
            queries, cache[s, :, :head_dim], (((1,), (1,)), ((), ())), preferred_element_type=F32
        )
        live = (place == s) & (position < lengths[s])
        scores = jnp.where(live, found * scale, scores)
    top = jnp.maximum(jnp.max(scores, 1, keepdims=True), own)
    weights = jnp.where(scores > 0.5 * masked_fill, jnp.exp(scores - top), 0.0)
    own_weight = jnp.where(block == 0, jnp.exp(own - top), 0.0)
    denom = jnp.sum(weights, 1, keepdims=True) + own_weight
    numer = own_weight * vs[...]
    for s in range(seq_dev):
        mine = jnp.where(place == s, weights, 0.0).astype(BF16)
        numer += jnp.dot(mine, cache[s, :, head_dim:], preferred_element_type=F32)

    lane = iota((many, head_dim), 1)
    terms = jnp.zeros((many, head_dim), F32)
    for j, term in enumerate(thirds(top) + thirds(denom)):
        terms = jnp.where((lane == place * 6 + j) & (place < seq_dev), term, terms)
    spare = jnp.zeros((many, head_dim), F32)
    for step in range(1, each):
        spare += pltpu.roll(terms, step, 0)
    out = jnp.where(place == seq_dev, spare, numer)
    count = heads_dev * each
    for c in range(cols):
        piece = out[c * count : (c + 1) * count].astype(BF16)
        for i in range(gx):
            sent[i * cols + c] = piece


def hidden_kernel(gx, seq_dev, stats, *refs):
    parts, hidden = refs[:-1], refs[-1]
    rows, ff_dev = hidden.shape
    each = seq_dev + 1
    place = lax.axis_index("gx")
    slab = min(ff_dev, 1024)
    inverse = stats[gx][:, :1]
    shifts = [stats[place ^ step][:, :1] for step in range(gx)]
    for start in range(0, ff_dev, slab):
        sums = []
        for base in (start, ff_dev + start):
            total = 0.0
            for step in range(gx):
                part = parts[step][:, base : base + slab].astype(F32)
                total += part + shifts[step] * part[seq_dev : each]
            sums.append(total * inverse)
        gate, upward = sums
        hidden[:, start : start + slab] = (gate / (1.0 + jnp.exp(-gate)) * upward).astype(BF16)


def out_kernel(dims, got, out_weight, partial, total, share, att):
    gx, gy, gz, seq_dev = dims
    each = seq_dev + 1
    count, head_dim = got.shape[1:]
    heads_dev = count // each
    place = iota((count, 1), 0) % each
    lanes = min(128, head_dim)
    for a in range(gy):
        values, tops, denoms = [], [], []
        for i in range(gx):
            for b in range(gz):
                piece = got[(i * gy + a) * gz + b].astype(F32)
                spare = jnp.where(place == seq_dev, piece[:, :lanes], 0.0)
                marks = spare
                for step in range(1, each):
                    marks += pltpu.roll(spare, count - step, 0)
                values.append(piece)
                tops.append(from_lanes(marks, place * 6, 3))
                denoms.append(from_lanes(marks, place * 6 + 3, 3))
        top = functools.reduce(jnp.maximum, tops)
        numer, denom = 0.0, 0.0
        for value, mine, part in zip(values, tops, denoms):
            factor = jnp.exp(mine - top)
            numer += value * factor
            denom += part * factor
        ratio = jnp.where(place < seq_dev, numer / jnp.where(place < seq_dev, denom, 1.0), 0.0)
        for h in range(heads_dev):
            att[a * each : (a + 1) * each, h * head_dim : (h + 1) * head_dim] = ratio[
                h * each : (h + 1) * each
            ]
    result = partial[...] + jnp.dot(
        att[...].astype(BF16), out_weight[...], preferred_element_type=F32
    )
    for a in range(gy):
        total[a * seq_dev : (a + 1) * seq_dev, :] = result[a * each : a * each + seq_dev]
    share[...] = total[...].astype(BF16)


def from_others(values, axis):
    size = lax.axis_size(axis)
    return [
        lax.ppermute(values, axis, [(place, place ^ step) for place in range(size)])
        for step in range(1, size)
    ]


def body(
    tokens,
    norm_gain,
    q_weight,
    kv_weight,
    out_weight,
    gate_weight,
    up_weight,
    down_weight,
    kv_cache,
    lengths,
):
    gx, gy, gz = (lax.axis_size(axis) for axis in PART)
    cols = gy * gz
    seqs, width = tokens.shape
    seq_dev = lengths.shape[0]
    head_dim = kv_weight.shape[1] // 2
    q_dev = q_weight.shape[1]
    heads_dev = q_dev // head_dim
    kv_dev = kv_weight.shape[1] // cols
    ff_dev = gate_weight.shape[1]
    each = seq_dev + 1
    rows = gy * each
    many = heads_dev * cols * each
    lanes = -(-seqs * 6 // 128) * 128
    pieces = max(1, width // 256)

    kv_own = kv_weight
    if kv_dev % 128:
        col = lax.axis_index(("gy", "gz"))
        kv_own = lax.dynamic_slice_in_dim(kv_weight, col * kv_dev, kv_dev, 1)
    sent, lhs = pl.pallas_call(
        functools.partial(first_kernel, (gx, gy, gz, seq_dev, pieces)),
        out_shape=(
            jax.ShapeDtypeStruct((gx * cols, each, q_dev + kv_dev + lanes), BF16),
            jax.ShapeDtypeStruct((rows, width), BF16),
        ),
        in_specs=[VMEM, VMEM, ANY, ANY],
        out_specs=(VMEM, VMEM),
        scratch_shapes=[
            pltpu.VMEM((rows, width), F32),
            pltpu.VMEM((width, q_dev), BF16),
            pltpu.VMEM((width, kv_dev), BF16),
            pltpu.SemaphoreType.DMA((pieces,)),
            pltpu.SemaphoreType.DMA,
        ],
        compiler_params=params(),
        cost_estimate=cost(2 * rows * width * (q_dev + kv_dev), 2 * width * (q_dev + kv_dev)),
        name="norm_query",
    )(tokens, norm_gain[None, :], q_weight, kv_own)
    got = lax.all_to_all(sent, PART, split_axis=0, concat_axis=0, tiled=True)

    gate_part = jnp.dot(lhs, gate_weight, preferred_element_type=F32).astype(BF16)
    up_part = jnp.dot(lhs, up_weight, preferred_element_type=F32).astype(BF16)
    both = jnp.concatenate([gate_part, up_part], 1)
    if gx <= FEW:
        parts = [both] + from_others(both, "gx")
    else:
        gathered = lax.all_gather(both, "gx")
        here = lax.axis_index("gx")
        parts = [lax.dynamic_index_in_dim(gathered, here ^ step, 0, False) for step in range(gx)]

    angle = jnp.pad(angles(lengths, head_dim), ((0, 1), (0, 0)))
    tables = jnp.stack([jnp.cos(angle), jnp.sin(angle)])
    sent, new_kv, stats = pl.pallas_call(
        functools.partial(attention_kernel, (gx, gy, gz, seq_dev, q_dev, kv_dev, gx * width)),
        out_shape=(
            jax.ShapeDtypeStruct((gx * cols, heads_dev * each, head_dim), BF16),
            jax.ShapeDtypeStruct((seq_dev, 2 * head_dim), BF16),
            jax.ShapeDtypeStruct((gx + 1, rows, 128), F32),
        ),
        in_specs=[VMEM, VMEM, SMEM, VMEM],
        out_specs=(VMEM, VMEM, VMEM),
        scratch_shapes=[pltpu.VMEM((many, head_dim), F32)] * 3,
        compiler_params=params(),
        cost_estimate=cost(4 * many * head_dim * seq_dev * kv_cache.shape[1], 2 * kv_cache.size),
        name="attention",
    )(got, kv_cache, lengths, tables)
    got = lax.all_to_all(sent, PART, split_axis=0, concat_axis=0, tiled=True)

    hidden = pl.pallas_call(
        functools.partial(hidden_kernel, gx, seq_dev),
        out_shape=jax.ShapeDtypeStruct((rows, ff_dev), BF16),
        in_specs=[VMEM] * (gx + 1),
        out_specs=VMEM,
        compiler_params=params(),
        cost_estimate=cost(16 * rows * ff_dev, 4 * gx * rows * ff_dev),
        name="hidden",
    )(stats, *parts)
    partial = jnp.dot(hidden, down_weight, preferred_element_type=F32)

    total, share = pl.pallas_call(
        functools.partial(out_kernel, (gx, gy, gz, seq_dev)),
        out_shape=(
            jax.ShapeDtypeStruct((seqs, width), F32),
            jax.ShapeDtypeStruct((seqs, width), BF16),
        ),
        in_specs=[VMEM] * 3,
        out_specs=(VMEM, VMEM),
        scratch_shapes=[pltpu.VMEM((rows, q_dev), F32)],
        compiler_params=params(),
        cost_estimate=cost(2 * rows * q_dev * width, 2 * q_dev * width),
        name="out_projection",
    )(got, out_weight, partial)
    for other in from_others(share, ("gy", "gz")):
        total = total + other.astype(F32)
    mixed = (tokens.astype(F32) + total).astype(BF16)
    return (mixed, new_kv)


def solution(mesh):
    in_specs = (
        P("group", "gx"),
        P("gx"),
        P("gx", ("gy", "gz")),
        P("gx", None),
        P(("gy", "gz"), "gx"),
        P("gx", ("gy", "gz")),
        P("gx", ("gy", "gz")),
        P(("gy", "gz"), "gx"),
        P(("group", "gy"), ("gx", "gz"), None),
        P(("group", "gy")),
    )
    out_specs = (P("group", "gx"), P(("group", "gy"), None))
    return jax.shard_map(body, mesh=mesh, in_specs=in_specs, out_specs=out_specs, check_vma=False)
```

```python
import functools

import jax
import jax.numpy as jnp
from jax import lax
from jax.experimental import pallas as pl
from jax.experimental.pallas import tpu as pltpu
from jax.sharding import PartitionSpec as P

epsilon = 1e-05
masked_fill = -1e30
rotary_base = 10000.0
PART = ("gx", "gy", "gz")
FEW = 8
LIMIT = 3
F32 = jnp.float32
BF16 = jnp.bfloat16
VMEM = pl.BlockSpec(memory_space=pltpu.VMEM)
SMEM = pl.BlockSpec(memory_space=pltpu.SMEM)
ANY = pl.BlockSpec(memory_space=pl.ANY)
HBM = pl.BlockSpec(memory_space=pltpu.HBM)
MIB = 2**20


def iota(shape, dim):
    return lax.broadcasted_iota(jnp.int32, shape, dim)


def thirds(values):
    high = values.astype(BF16).astype(F32)
    rest = values - high
    middle = rest.astype(BF16).astype(F32)
    return high, middle, rest - middle


def from_lanes(row, first, count):
    lane = iota(row.shape, 1)
    return jnp.sum(jnp.where((lane >= first) & (lane < first + count), row, 0.0), 1, keepdims=True)


def rotated_halves(values, cosine, sine):
    middle = values.shape[-1] // 2
    first, second = values[:, :middle], values[:, middle:]
    return jnp.concatenate(
        [first * cosine - second * sine, first * sine + second * cosine], 1
    )


def cost(flops, nbytes):
    return pl.CostEstimate(flops=int(flops), bytes_accessed=int(nbytes), transcendentals=0)


def params(mebibytes):
    return pltpu.CompilerParams(vmem_limit_bytes=mebibytes * MIB)


def exponent_kernel(table):
    table[...] = iota(table.shape, 1).astype(F32) / -table.shape[1]


def first_kernel(dims, tokens, gain, q_weight, kv_weight, after, sums, lhs, rows):
    gy, gz, seq_dev, kv_dev = dims
    inputs = tokens[...].astype(F32)
    seqs, width = inputs.shape
    mean = jnp.sum(inputs, 1, keepdims=True) / width
    centred = inputs - mean
    square = jnp.sum(centred * centred, 1, keepdims=True)
    scaled = centred * gain[...]
    each = seq_dev + 1
    for a in range(gy):
        rows[a * each : a * each + seq_dev, :] = scaled[a * seq_dev : (a + 1) * seq_dev]
        rows[a * each + seq_dev : (a + 1) * each, :] = gain[...]
    lhs[...] = rows[...].astype(BF16)

    lanes = sums.shape[1] - q_weight.shape[1] - kv_dev
    lane = iota((seqs, lanes), 1)
    first = iota((seqs, lanes), 0) * 6
    marks = jnp.zeros((seqs, lanes), F32)
    for place, term in enumerate(thirds(mean) + thirds(square)):
        marks = jnp.where(lane == first + place, term, marks)
    marks = jnp.broadcast_to(jnp.sum(marks, 0, keepdims=True), (gy * each, lanes))

    values = lhs[...]
    query = jnp.dot(values, q_weight[...], preferred_element_type=F32)
    kv_own = kv_weight[...]
    if kv_weight.shape[1] != kv_dev:
        col = lax.axis_index("gy") * gz + lax.axis_index("gz")
        kv_own = kv_weight[:, pl.ds(pl.multiple_of(col * kv_dev, kv_dev), kv_dev)]
    keyval = jnp.dot(values, kv_own, preferred_element_type=F32)
    sums[...] = jnp.concatenate([query, keyval, marks], 1).astype(BF16)


def sum_kernel(dims, *refs):
    gx, gy, seq_dev, width, features = dims
    parts, (whole, stats) = refs[:gx], refs[gx:]
    each = seq_dev + 1
    rows = gy * each
    place = iota((rows, 1), 0)
    valid = place % each < seq_dev
    first = (place // each * seq_dev + place % each) * 6
    means, squares = [], 0.0
    for part in parts:
        marks = part[:, width:].astype(F32)
        means.append(jnp.where(valid, from_lanes(marks, first, 3), 0.0))
        squares += from_lanes(marks, first + 3, 3)
    center = sum(means) / gx
    shifts = [mean - center for mean in means]
    spread = squares / features + sum(s * s for s in shifts) / gx
    inverse = jnp.where(valid, lax.rsqrt(spread + epsilon), 0.0)
    for step in range(gx):
        stats[step] = jnp.broadcast_to(shifts[step], stats.shape[1:])
    stats[gx] = jnp.broadcast_to(inverse, stats.shape[1:])
    whole[...] = (shifted_sum([p[:, :width] for p in parts], shifts, seq_dev) * inverse).astype(BF16)


def shifted_sum(parts, shifts, seq_dev):
    total = 0.0
    for part, shift in zip(parts, shifts):
        part = part.astype(F32)
        total += part + shift * part[seq_dev : seq_dev + 1]
    return total


def product(lhs, weight, store, slab=512):
    slab = min(slab, weight.shape[1])

    def step(index, _):
        part = pl.ds(pl.multiple_of(index * slab, slab), slab)
        store(part, jnp.dot(lhs, weight[:, part], preferred_element_type=F32))
        return 0

    lax.fori_loop(0, weight.shape[1] // slab, step, 0)


def partial_kernel(lhs, weight, *refs):
    sums = refs[-1]
    def store(part, value):
        sums[:, part] = value.astype(BF16)

    product(lhs[...], weight, store)


def attention_kernel(dims, *refs):
    gy, gz, seq_dev, q_dev, kv_dev = dims
    cols = gy * gz
    parts, (cache, lengths, tables, after) = refs[:cols], refs[cols : cols + 4]
    pieces, (new_kv, qs, ks, vs, kvs) = refs[cols + 4 : 2 * cols + 4], refs[2 * cols + 4 :]
    each = seq_dev + 1
    ctx_dev = cache.shape[1]
    head_dim = cache.shape[2] // 2
    heads_dev = q_dev // head_dim
    heads = heads_dev * cols
    row = lax.axis_index("gy")
    col = row * gz + lax.axis_index("gz")
    block = lax.axis_index("gx") * gz + lax.axis_index("gz")

    cosine, sine = tables[0], tables[1]
    for step in range(cols):
        part = parts[step][...].astype(F32)
        mine = part[:each]
        for a in range(1, gy):
            mine = jnp.where(row == a, part[a * each : (a + 1) * each], mine)
        kvs[step] = mine[:, q_dev:]
        for h in range(heads_dev):
            turned = rotated_halves(mine[:, h * head_dim : (h + 1) * head_dim], cosine, sine)
            head = step * heads_dev + h
            qs[head * each : (head + 1) * each, :] = turned
    keyval = jnp.concatenate([kvs[col ^ c] for c in range(cols)], 1)
    fresh = jnp.concatenate(
        [rotated_halves(keyval[:, :head_dim], cosine, sine), keyval[:, head_dim:]], 1
    ).astype(BF16)
    new_kv[...] = fresh[:seq_dev]
    fresh = fresh.astype(F32)
    for head in range(heads):
        ks[head * each : (head + 1) * each, :] = fresh[:, :head_dim]
        vs[head * each : (head + 1) * each, :] = fresh[:, head_dim:]

    many = heads * each
    scale = head_dim ** (-0.5)
    queries = qs[...].astype(BF16)
    own = jnp.sum(queries.astype(F32) * ks[...], 1, keepdims=True) * scale
    place = iota((many, 1), 0) % each
    position = block * ctx_dev + iota((many, ctx_dev), 1)
    scores = jnp.full((many, ctx_dev), masked_fill, F32)
    for s in range(seq_dev):
        found = lax.dot_general(
            queries, cache[s, :, :head_dim], (((1,), (1,)), ((), ())), preferred_element_type=F32
        )
        live = (place == s) & (position < lengths[s])
        scores = jnp.where(live, found * scale, scores)
    top = jnp.maximum(jnp.max(scores, 1, keepdims=True), own)
    weights = jnp.where(scores > 0.5 * masked_fill, jnp.exp(scores - top), 0.0)
    own_weight = jnp.where(block == 0, jnp.exp(own - top), 0.0)
    denom = jnp.sum(weights, 1, keepdims=True) + own_weight
    numer = own_weight * vs[...]
    for s in range(seq_dev):
        mine = jnp.where(place == s, weights, 0.0).astype(BF16)
        numer += jnp.dot(mine, cache[s, :, head_dim:], preferred_element_type=F32)

    lane = iota((many, head_dim), 1)
    terms = jnp.zeros((many, head_dim), F32)
    for j, term in enumerate(thirds(top) + thirds(denom)):
        terms = jnp.where((lane == place * 6 + j) & (place < seq_dev), term, terms)
    spare = jnp.zeros((many, head_dim), F32)
    for step in range(1, each):
        spare += pltpu.roll(terms, step, 0)
    out = jnp.where(place == seq_dev, spare, numer)
    count = heads_dev * each
    for step in range(cols):
        pieces[step][...] = out[step * count : (step + 1) * count].astype(BF16)


def down_kernel(dims, stats, *refs):
    gx, seq_dev = dims
    parts, (down, result, hidden) = refs[:gx], refs[gx:]
    rows, ff_dev = hidden.shape
    slab = min(ff_dev, 1024)
    inverse = stats[gx][:, :1]
    shifts = [stats[step][:, :1] for step in range(gx)]
    for start in range(0, ff_dev, slab):
        sums = []
        for base in (0, rows):
            found = [part[base : base + rows, start : start + slab] for part in parts]
            sums.append(shifted_sum(found, shifts, seq_dev) * inverse)
        gate, upward = sums
        hidden[:, start : start + slab] = (gate / (1.0 + jnp.exp(-gate)) * upward).astype(BF16)

    def store(part, value):
        result[:, part] = value

    product(hidden[...], down, store)


def out_kernel(dims, *refs):
    gx, gy, gz, seq_dev = dims
    parts, (out_weight, partial, total, share, turned, att) = refs[:gx], refs[gx:]
    each = seq_dev + 1
    count, head_dim = parts[0].shape[1:]
    heads_dev = count // each
    place = iota((count, 1), 0) % each
    lanes = min(128, head_dim)
    row = lax.axis_index("gy")
    for a in range(gy):
        values, tops, denoms = [], [], []
        for part in parts:
            for b in range(gz):
                piece = part[a * gz + b].astype(F32)
                spare = jnp.where(place == seq_dev, piece[:, :lanes], 0.0)
                marks = spare
                for step in range(1, each):
                    marks += pltpu.roll(spare, count - step, 0)
                values.append(piece)
                tops.append(from_lanes(marks, place * 6, 3))
                denoms.append(from_lanes(marks, place * 6 + 3, 3))
        top = functools.reduce(jnp.maximum, tops)
        numer, denom = 0.0, 0.0
        for value, mine, part in zip(values, tops, denoms):
            factor = jnp.exp(mine - top)
            numer += value * factor
            denom += part * factor
        ratio = jnp.where(place < seq_dev, numer / jnp.where(place < seq_dev, denom, 1.0), 0.0)
        for h in range(heads_dev):
            turned[row ^ a, :, h * head_dim : (h + 1) * head_dim] = ratio[
                h * each : (h + 1) * each
            ]
    for a in range(gy):
        att[a * each : (a + 1) * each, :] = turned[a]
    result = partial[...] + jnp.dot(
        att[...].astype(BF16), out_weight[...], preferred_element_type=F32
    )
    for a in range(gy):
        total[a * seq_dev : (a + 1) * seq_dev, :] = result[a * each : a * each + seq_dev]
    share[...] = total[...].astype(BF16)


def with_others(values, axis):
    size = lax.axis_size(axis)
    if size <= FEW:
        return [values] + [
            lax.ppermute(values, axis, [(place, place ^ step) for place in range(size)])
            for step in range(1, size)
        ]
    gathered = lax.all_gather(values, axis)
    here = lax.axis_index(axis)
    return [lax.dynamic_index_in_dim(gathered, here ^ step, 0, False) for step in range(size)]


def body(
    tokens,
    norm_gain,
    q_weight,
    kv_weight,
    out_weight,
    gate_weight,
    up_weight,
    down_weight,
    kv_cache,
    lengths,
):
    gx, gy, gz = (lax.axis_size(axis) for axis in PART)
    cols = gy * gz
    seqs, width = tokens.shape
    seq_dev = lengths.shape[0]
    head_dim = kv_weight.shape[1] // 2
    q_dev = q_weight.shape[1]
    heads_dev = q_dev // head_dim
    kv_dev = kv_weight.shape[1] // cols
    ff_dev = gate_weight.shape[1]
    each = seq_dev + 1
    rows = gy * each
    many = heads_dev * cols * each
    lanes = -(-seqs * 6 // 128) * 128

    kv_own = kv_weight
    if kv_dev % 128:
        col = lax.axis_index(("gy", "gz"))
        kv_own = lax.dynamic_slice_in_dim(kv_weight, col * kv_dev, kv_dev, 1)
    exponents = pl.pallas_call(
        exponent_kernel,
        out_shape=jax.ShapeDtypeStruct((1, head_dim // 2), F32),
        out_specs=VMEM,
        compiler_params=params(LIMIT),
        cost_estimate=cost(7e9, 0),
        name="exponents",
    )()
    sums, lhs = pl.pallas_call(
        functools.partial(first_kernel, (gy, gz, seq_dev, kv_dev)),
        out_shape=(
            jax.ShapeDtypeStruct((rows, q_dev + kv_dev + lanes), BF16),
            jax.ShapeDtypeStruct((rows, width), BF16),
        ),
        in_specs=[VMEM] * 4 + [ANY],
        out_specs=(VMEM, VMEM),
        scratch_shapes=[pltpu.VMEM((rows, width), F32)],
        compiler_params=params(LIMIT),
        cost_estimate=cost(7e9, 0),
        name="norm_query",
    )(tokens, norm_gain[None, :], q_weight, kv_own, exponents)
    sums = with_others(sums, "gx")
    query, stats = pl.pallas_call(
        functools.partial(sum_kernel, (gx, gy, seq_dev, q_dev + kv_dev, gx * width)),
        out_shape=(
            jax.ShapeDtypeStruct((rows, q_dev + kv_dev), BF16),
            jax.ShapeDtypeStruct((gx + 1, rows, 128), F32),
        ),
        in_specs=[VMEM] * gx,
        out_specs=(VMEM, VMEM),
        compiler_params=params(LIMIT),
        name="query_sum",
    )(*sums)
    queries = with_others(query, ("gy", "gz"))

    def partial_sums(weight, name, *after):
        return pl.pallas_call(
            partial_kernel,
            out_shape=jax.ShapeDtypeStruct((rows, ff_dev), BF16),
            in_specs=[VMEM, VMEM] + [ANY] * len(after),
            out_specs=VMEM,
            compiler_params=params(LIMIT),
            cost_estimate=cost(6e9, 16.8e6),
            name=name,
        )(lhs, weight, *after)

    gate = partial_sums(gate_weight, "gate")
    both = jnp.concatenate([gate, partial_sums(up_weight, "up", query)], 0)
    parts = with_others(both, "gx")

    angle = lengths.astype(F32)[:, None] * rotary_base**exponents
    angle = jnp.pad(angle, ((0, 1), (0, 0)))
    tables = jnp.stack([jnp.cos(angle), jnp.sin(angle)])
    piece = jax.ShapeDtypeStruct((heads_dev * each, head_dim), BF16)
    *pieces, new_kv = pl.pallas_call(
        functools.partial(attention_kernel, (gy, gz, seq_dev, q_dev, kv_dev)),
        out_shape=(piece,) * cols + (jax.ShapeDtypeStruct((seq_dev, 2 * head_dim), BF16),),
        in_specs=[VMEM] * (cols + 1) + [SMEM, VMEM, ANY],
        out_specs=(VMEM,) * (cols + 1),
        scratch_shapes=[pltpu.VMEM((many, head_dim), F32)] * 3
        + [pltpu.VMEM((cols, each, kv_dev), F32)],
        compiler_params=params(LIMIT),
        cost_estimate=cost(7e9, 2e6),
        name="attention",
    )(*queries, kv_cache, lengths, tables, both)
    pieces = pieces[:1] + [
        lax.ppermute(pieces[step], ("gy", "gz"), [(place, place ^ step) for place in range(cols)])
        for step in range(1, cols)
    ]
    pieces = with_others(jnp.stack(pieces), "gx")

    partial = pl.pallas_call(
        functools.partial(down_kernel, (gx, seq_dev)),
        out_shape=jax.ShapeDtypeStruct((rows, width), F32),
        in_specs=[VMEM] * (gx + 2),
        out_specs=VMEM,
        scratch_shapes=[pltpu.VMEM((rows, ff_dev), BF16)],
        compiler_params=params(LIMIT),
        cost_estimate=cost(4e9, 16.8e6),
        name="hidden_down",
    )(stats, *parts, down_weight)
    total, share = pl.pallas_call(
        functools.partial(out_kernel, (gx, gy, gz, seq_dev)),
        out_shape=(
            jax.ShapeDtypeStruct((seqs, width), F32),
            jax.ShapeDtypeStruct((seqs, width), BF16),
        ),
        in_specs=[VMEM] * (gx + 2),
        out_specs=(VMEM, VMEM),
        scratch_shapes=[pltpu.VMEM((gy, each, q_dev), F32), pltpu.VMEM((rows, q_dev), F32)],
        compiler_params=params(LIMIT),
        cost_estimate=cost(1e9, 4e6),
        name="out_projection",
    )(*pieces, out_weight, partial)
    for other in with_others(share, ("gy", "gz"))[1:]:
        total = total + other.astype(F32)
    mixed = (tokens.astype(F32) + total).astype(BF16)
    return (mixed, new_kv)


def solution(mesh):
    in_specs = (
        P("group", "gx"),
        P("gx"),
        P("gx", ("gy", "gz")),
        P("gx", None),
        P(("gy", "gz"), "gx"),
        P("gx", ("gy", "gz")),
        P("gx", ("gy", "gz")),
        P(("gy", "gz"), "gx"),
        P(("group", "gy"), ("gx", "gz"), None),
        P(("group", "gy")),
    )
    out_specs = (P("group", "gx"), P(("group", "gy"), None))
    return jax.shard_map(body, mesh=mesh, in_specs=in_specs, out_specs=out_specs, check_vma=False)
```

```python
import functools

import jax
import jax.numpy as jnp
from jax import lax
from jax.experimental import pallas as pl
from jax.experimental.pallas import tpu as pltpu
from jax.sharding import PartitionSpec as P

epsilon = 1e-05
masked_fill = -1e30
rotary_base = 10000.0
FEW = 8
LIMIT = 3
F32 = jnp.float32
BF16 = jnp.bfloat16
VMEM = pl.BlockSpec(memory_space=pltpu.VMEM)
SMEM = pl.BlockSpec(memory_space=pltpu.SMEM)
ANY = pl.BlockSpec(memory_space=pl.ANY)
HBM = pl.BlockSpec(memory_space=pltpu.HBM)
MIB = 2**20


def iota(shape, dim):
    return lax.broadcasted_iota(jnp.int32, shape, dim)


def thirds(values):
    high = values.astype(BF16).astype(F32)
    rest = values - high
    middle = rest.astype(BF16).astype(F32)
    return high, middle, rest - middle


def from_lanes(row, first, count):
    lane = iota(row.shape, 1)
    return jnp.sum(jnp.where((lane >= first) & (lane < first + count), row, 0.0), 1, keepdims=True)


def rotated_halves(values, cosine, sine):
    middle = values.shape[-1] // 2
    first, second = values[:, :middle], values[:, middle:]
    return jnp.concatenate(
        [first * cosine - second * sine, first * sine + second * cosine], 1
    )


def cost(flops, nbytes):
    return pl.CostEstimate(flops=int(flops), bytes_accessed=int(nbytes), transcendentals=0)


def params(mebibytes):
    return pltpu.CompilerParams(vmem_limit_bytes=mebibytes * MIB)


def exponent_kernel(table):
    table[...] = iota(table.shape, 1).astype(F32) / -table.shape[1]


def first_kernel(dims, tokens, gain, q_weight, kv_weight, after, sums, lhs, rows):
    gy, seq_dev = dims
    inputs = tokens[...].astype(F32)
    seqs, width = inputs.shape
    mean = jnp.sum(inputs, 1, keepdims=True) / width
    centred = inputs - mean
    square = jnp.sum(centred * centred, 1, keepdims=True)
    scaled = centred * gain[...]
    each = seq_dev + 1
    for a in range(gy):
        rows[a * each : a * each + seq_dev, :] = scaled[a * seq_dev : (a + 1) * seq_dev]
        rows[a * each + seq_dev : (a + 1) * each, :] = gain[...]
    lhs[...] = rows[...].astype(BF16)

    lanes = sums.shape[1] - q_weight.shape[1] - kv_weight.shape[1]
    lane = iota((seqs, lanes), 1)
    first = iota((seqs, lanes), 0) * 6
    marks = jnp.zeros((seqs, lanes), F32)
    for place, term in enumerate(thirds(mean) + thirds(square)):
        marks = jnp.where(lane == first + place, term, marks)
    marks = jnp.broadcast_to(jnp.sum(marks, 0, keepdims=True), (gy * each, lanes))

    values = lhs[...]
    query = jnp.dot(values, q_weight[...], preferred_element_type=F32)
    keyval = jnp.dot(values, kv_weight[...], preferred_element_type=F32)
    sums[...] = jnp.concatenate([query, keyval, marks], 1).astype(BF16)


def centring(dims, parts, width):
    gx, gy, seq_dev, features = dims
    each = seq_dev + 1
    place = iota((gy * each, 1), 0)
    valid = place % each < seq_dev
    first = (place // each * seq_dev + place % each) * 6
    means, squares = [], 0.0
    for part in parts:
        marks = part[:, width:].astype(F32)
        means.append(jnp.where(valid, from_lanes(marks, first, 3), 0.0))
        squares += from_lanes(marks, first + 3, 3)
    center = sum(means) / gx
    shifts = [mean - center for mean in means]
    spread = squares / features + sum(s * s for s in shifts) / gx
    return shifts, jnp.where(valid, lax.rsqrt(spread + epsilon), 0.0)


def shifted_sum(parts, shifts, seq_dev):
    total = 0.0
    for part, shift in zip(parts, shifts):
        part = part.astype(F32)
        total += part + shift * part[seq_dev : seq_dev + 1]
    return total


def product(lhs, weight, store, slab=512):
    slab = min(slab, weight.shape[1])

    def step(index, _):
        part = pl.ds(pl.multiple_of(index * slab, slab), slab)
        store(part, jnp.dot(lhs, weight[:, part], preferred_element_type=F32))
        return 0

    lax.fori_loop(0, weight.shape[1] // slab, step, 0)


def gate_kernel(lhs, weight, sums):
    def store(part, value):
        sums[:, part] = value.astype(BF16)

    product(lhs[...], weight, store)


def up_kernel(lhs, weight, gate, after, both):
    rows = lhs.shape[0]
    both[:rows, :] = gate[...]

    def store(part, value):
        both[rows:, part] = value.astype(BF16)

    product(lhs[...], weight, store)


def query_kernel(dims, *refs):
    gx, gy, seq_dev, q_dev, features = dims
    parts, (query, keyval, stats) = refs[:gx], refs[gx:]
    width = q_dev + keyval.shape[1]
    shifts, inverse = centring((gx, gy, seq_dev, features), parts, width)
    for step in range(gx):
        stats[step] = jnp.broadcast_to(shifts[step], stats.shape[1:])
    stats[gx] = jnp.broadcast_to(inverse, stats.shape[1:])
    whole = shifted_sum([part[:, :width] for part in parts], shifts, seq_dev) * inverse
    query[...] = whole[:, :q_dev].astype(BF16)
    keyval[...] = whole[:, q_dev:]


def attention_kernel(dims, *refs):
    gy, gz, seq_dev = dims
    each = seq_dev + 1
    parts, refs = refs[:gy], refs[gy:]
    caches, refs = refs[:gz], refs[gz:]
    lengths, keyval, tables, after = refs[:4]
    pieces, (new_kv, qs, ks, vs) = refs[4 : 4 + gy], refs[4 + gy :]
    ctx_dev, head_dim = caches[0].shape[1], caches[0].shape[2] // 2
    heads_dev = parts[0].shape[1] // head_dim
    row = lax.axis_index("gy")

    def own_rows(values):
        mine = values[:each]
        for a in range(1, gy):
            mine = jnp.where(row == a, values[a * each : (a + 1) * each], mine)
        return mine

    cosine, sine = tables[0], tables[1]
    fresh = own_rows(keyval[...])
    fresh = jnp.concatenate(
        [rotated_halves(fresh[:, :head_dim], cosine, sine), fresh[:, head_dim:]], 1
    ).astype(BF16)
    new_kv[...] = fresh[:seq_dev]
    fresh = fresh.astype(F32)
    for da in range(gy):
        query = own_rows(parts[da][...].astype(F32))
        for h in range(heads_dev):
            start = (da * heads_dev + h) * each
            part = slice(start, start + each)
            qs[part, :] = rotated_halves(query[:, h * head_dim : (h + 1) * head_dim], cosine, sine)
            ks[part, :] = fresh[:, :head_dim]
            vs[part, :] = fresh[:, head_dim:]

    count = heads_dev * each
    many = gy * count
    scale = head_dim ** (-0.5)
    queries = qs[...].astype(BF16)
    own = jnp.sum(queries.astype(F32) * ks[...], 1, keepdims=True) * scale
    sequence = iota((many, 1), 0) % each
    scores = []
    for db in range(gz):
        block = lax.axis_index("gx") * gz + (lax.axis_index("gz") ^ db)
        positions = block * ctx_dev + iota((many, ctx_dev), 1)
        found = jnp.full((many, ctx_dev), masked_fill, F32)
        for s in range(seq_dev):
            value = lax.dot_general(
                queries,
                caches[db][s, :, :head_dim],
                (((1,), (1,)), ((), ())),
                preferred_element_type=F32,
            )
            found = jnp.where((positions < lengths[s]) & (sequence == s), value * scale, found)
        scores.append(found)
    top = own
    for found in scores:
        top = jnp.maximum(top, jnp.max(found, 1, keepdims=True))
    own_weight = jnp.where(lax.axis_index("gx") == 0, jnp.exp(own - top), 0.0)
    denom = own_weight
    numer = own_weight * vs[...]
    for db in range(gz):
        weights = jnp.where(scores[db] > 0.5 * masked_fill, jnp.exp(scores[db] - top), 0.0)
        denom += jnp.sum(weights, 1, keepdims=True)
        for s in range(seq_dev):
            mine = jnp.where(sequence == s, weights, 0.0).astype(BF16)
            numer += jnp.dot(mine, caches[db][s, :, head_dim:], preferred_element_type=F32)

    lane = iota((many, head_dim), 1)
    terms = jnp.zeros((many, head_dim), F32)
    for j, term in enumerate(thirds(top) + thirds(denom)):
        terms = jnp.where((lane == sequence * 6 + j) & (sequence < seq_dev), term, terms)
    spare = jnp.zeros((many, head_dim), F32)
    for step in range(1, each):
        spare += pltpu.roll(terms, step, 0)
    out = jnp.where(sequence == seq_dev, spare, numer)
    for da in range(gy):
        pieces[da][...] = out[da * count : (da + 1) * count].astype(BF16)


def down_kernel(dims, stats, *refs):
    gx, seq_dev = dims
    parts, (down, result, hidden) = refs[:gx], refs[gx:]
    rows, ff_dev = hidden.shape
    slab = min(ff_dev, 1024)
    inverse = stats[gx][:, :1]
    shifts = [stats[step][:, :1] for step in range(gx)]
    for start in range(0, ff_dev, slab):
        sums = []
        for base in (0, rows):
            found = [part[base : base + rows, start : start + slab] for part in parts]
            sums.append(shifted_sum(found, shifts, seq_dev) * inverse)
        gate, upward = sums
        hidden[:, start : start + slab] = (gate / (1.0 + jnp.exp(-gate)) * upward).astype(BF16)

    def store(part, value):
        result[:, part] = value

    product(hidden[...], down, store)


def out_kernel(dims, *refs):
    gx, gy, seq_dev = dims
    parts, (out_weight, partial, total, share, turned, att) = refs[:gx], refs[gx:]
    each = seq_dev + 1
    count, head_dim = parts[0].shape[1:]
    sequence = iota((count, 1), 0) % each
    valid = sequence < seq_dev
    lanes = min(128, head_dim)
    row = lax.axis_index("gy")
    for da in range(gy):
        values, tops, denoms = [], [], []
        for part in parts:
            piece = part[da].astype(F32)
            spare = jnp.where(valid, 0.0, piece[:, :lanes])
            marks = spare
            for step in range(1, each):
                marks += pltpu.roll(spare, count - step, 0)
            values.append(piece)
            tops.append(from_lanes(marks, sequence * 6, 3))
            denoms.append(from_lanes(marks, sequence * 6 + 3, 3))
        top = functools.reduce(jnp.maximum, tops)
        numer, denom = 0.0, 0.0
        for value, mine, part in zip(values, tops, denoms):
            factor = jnp.exp(mine - top)
            numer += value * factor
            denom += part * factor
        ratio = jnp.where(valid, numer / jnp.where(valid, denom, 1.0), 0.0)
        for h in range(count // each):
            turned[row ^ da, :, h * head_dim : (h + 1) * head_dim] = ratio[
                h * each : (h + 1) * each
            ]
    for a in range(gy):
        att[a * each : (a + 1) * each, :] = turned[a]
    result = partial[...] + jnp.dot(
        att[...].astype(BF16), out_weight[...], preferred_element_type=F32
    )
    for a in range(gy):
        total[a * seq_dev : (a + 1) * seq_dev, :] = result[a * each : a * each + seq_dev]
    share[...] = total[...].astype(BF16)


def with_others(values, axis):
    size = lax.axis_size(axis)
    if size <= FEW:
        return [values] + [
            lax.ppermute(values, axis, [(place, place ^ step) for place in range(size)])
            for step in range(1, size)
        ]
    gathered = lax.all_gather(values, axis)
    here = lax.axis_index(axis)
    return [lax.dynamic_index_in_dim(gathered, here ^ step, 0, False) for step in range(size)]


def body(
    tokens,
    norm_gain,
    q_weight,
    kv_weight,
    out_weight,
    gate_weight,
    up_weight,
    down_weight,
    kv_cache,
    lengths,
):
    gx, gy, gz = (lax.axis_size(axis) for axis in ("gx", "gy", "gz"))
    seqs, width = tokens.shape
    seq_dev = lengths.shape[0]
    head_dim = kv_weight.shape[1] // 2
    q_dev = q_weight.shape[1]
    ff_dev = gate_weight.shape[1]
    each = seq_dev + 1
    rows = gy * each
    count = q_dev // head_dim * each
    lanes = -(-seqs * 6 // 128) * 128

    caches = with_others(kv_cache, "gz")

    exponents = pl.pallas_call(
        exponent_kernel,
        out_shape=jax.ShapeDtypeStruct((1, head_dim // 2), F32),
        out_specs=VMEM,
        compiler_params=params(LIMIT),
        cost_estimate=cost(7e9, 0),
        name="exponents",
    )()
    sums, lhs = pl.pallas_call(
        functools.partial(first_kernel, (gy, seq_dev)),
        out_shape=(
            jax.ShapeDtypeStruct((rows, q_dev + 2 * head_dim + lanes), BF16),
            jax.ShapeDtypeStruct((rows, width), BF16),
        ),
        in_specs=[VMEM] * 4 + [ANY],
        out_specs=(VMEM, VMEM),
        scratch_shapes=[pltpu.VMEM((rows, width), F32)],
        compiler_params=params(LIMIT),
        cost_estimate=cost(7e9, 0),
        name="norm_query",
    )(tokens, norm_gain[None, :], q_weight, kv_weight, exponents)
    sums = with_others(sums, "gx")

    gate = pl.pallas_call(
        gate_kernel,
        out_shape=jax.ShapeDtypeStruct((rows, ff_dev), BF16),
        in_specs=[VMEM, VMEM],
        out_specs=VMEM,
        compiler_params=params(LIMIT),
        cost_estimate=cost(6e9, 16.8e6),
        name="gate",
    )(lhs, gate_weight)
    query, keyval, stats = pl.pallas_call(
        functools.partial(query_kernel, (gx, gy, seq_dev, q_dev, gx * width)),
        out_shape=(
            jax.ShapeDtypeStruct((rows, q_dev), BF16),
            jax.ShapeDtypeStruct((rows, 2 * head_dim), F32),
            jax.ShapeDtypeStruct((gx + 1, rows, 128), F32),
        ),
        in_specs=[VMEM] * gx,
        out_specs=(VMEM,) * 3,
        compiler_params=params(LIMIT),
        cost_estimate=cost(1e8, 1e5),
        name="query_sum",
    )(*sums)
    queries = with_others(query, "gy")
    both = pl.pallas_call(
        up_kernel,
        out_shape=jax.ShapeDtypeStruct((2 * rows, ff_dev), BF16),
        in_specs=[VMEM] * 3 + [ANY],
        out_specs=VMEM,
        compiler_params=params(LIMIT),
        cost_estimate=cost(6e9, 16.8e6),
        name="up",
    )(lhs, up_weight, gate, query)
    parts = with_others(both, "gx")

    angle = lengths.astype(F32)[:, None] * rotary_base**exponents
    angle = jnp.pad(angle, ((0, 1), (0, 0)))
    tables = jnp.stack([jnp.cos(angle), jnp.sin(angle)])
    *pieces, new_kv = pl.pallas_call(
        functools.partial(attention_kernel, (gy, gz, seq_dev)),
        out_shape=(jax.ShapeDtypeStruct((count, head_dim), BF16),) * gy
        + (jax.ShapeDtypeStruct((seq_dev, 2 * head_dim), BF16),),
        in_specs=[VMEM] * (gz + gy) + [SMEM, VMEM, VMEM, ANY],
        out_specs=(VMEM,) * (gy + 1),
        scratch_shapes=[pltpu.VMEM((gy * count, head_dim), F32)] * 3,
        compiler_params=params(LIMIT),
        cost_estimate=cost(7e9, 2e6),
        name="attention",
    )(*queries, *caches, lengths, keyval, tables, both)
    pieces = pieces[:1] + [
        lax.ppermute(pieces[step], "gy", [(place, place ^ step) for place in range(gy)])
        for step in range(1, gy)
    ]
    pieces = with_others(jnp.stack(pieces), "gx")

    partial = pl.pallas_call(
        functools.partial(down_kernel, (gx, seq_dev)),
        out_shape=jax.ShapeDtypeStruct((rows, width), F32),
        in_specs=[VMEM] * (gx + 2),
        out_specs=VMEM,
        scratch_shapes=[pltpu.VMEM((rows, ff_dev), BF16)],
        compiler_params=params(LIMIT),
        cost_estimate=cost(4e9, 16.8e6),
        name="hidden_down",
    )(stats, *parts, down_weight)
    total, share = pl.pallas_call(
        functools.partial(out_kernel, (gx, gy, seq_dev)),
        out_shape=(
            jax.ShapeDtypeStruct((seqs, width), F32),
            jax.ShapeDtypeStruct((seqs, width), BF16),
        ),
        in_specs=[VMEM] * (gx + 2),
        out_specs=(VMEM, VMEM),
        scratch_shapes=[pltpu.VMEM((gy, each, q_dev), F32), pltpu.VMEM((rows, q_dev), F32)],
        compiler_params=params(LIMIT if gx <= FEW else 4 * LIMIT),
        cost_estimate=cost(1e9, 4e6),
        name="out_projection",
    )(*pieces, out_weight, partial)
    for other in with_others(share, ("gy", "gz"))[1:]:
        total = total + other.astype(F32)
    mixed = (tokens.astype(F32) + total).astype(BF16)
    return (mixed, new_kv)


def solution(mesh):
    in_specs = (
        P("group", "gx"),
        P("gx"),
        P("gx", ("gy", "gz")),
        P("gx", None),
        P(("gy", "gz"), "gx"),
        P("gx", ("gy", "gz")),
        P("gx", ("gy", "gz")),
        P(("gy", "gz"), "gx"),
        P(("group", "gy"), ("gx", "gz"), None),
        P(("group", "gy")),
    )
    out_specs = (P("group", "gx"), P(("group", "gy"), None))
    return jax.shard_map(body, mesh=mesh, in_specs=in_specs, out_specs=out_specs, check_vma=False)
```

```python
import functools

import jax
import jax.numpy as jnp
from jax import lax
from jax.experimental import pallas as pl
from jax.experimental.pallas import tpu as pltpu
from jax.sharding import PartitionSpec as P

epsilon = 1e-05
masked_fill = -1e30
rotary_base = 10000.0
FEW = 8
LIMIT = 3
F32 = jnp.float32
BF16 = jnp.bfloat16
VMEM = pl.BlockSpec(memory_space=pltpu.VMEM)
SMEM = pl.BlockSpec(memory_space=pltpu.SMEM)
ANY = pl.BlockSpec(memory_space=pl.ANY)
HBM = pl.BlockSpec(memory_space=pltpu.HBM)
MIB = 2**20


def iota(shape, dim):
    return lax.broadcasted_iota(jnp.int32, shape, dim)


def thirds(values):
    high = values.astype(BF16).astype(F32)
    rest = values - high
    middle = rest.astype(BF16).astype(F32)
    return high, middle, rest - middle


def from_lanes(row, first, count):
    lane = iota(row.shape, 1)
    return jnp.sum(jnp.where((lane >= first) & (lane < first + count), row, 0.0), 1, keepdims=True)


def rotated_halves(values, cosine, sine):
    middle = values.shape[-1] // 2
    first, second = values[:, :middle], values[:, middle:]
    return jnp.concatenate(
        [first * cosine - second * sine, first * sine + second * cosine], 1
    )


def cost(flops, nbytes):
    return pl.CostEstimate(flops=int(flops), bytes_accessed=int(nbytes), transcendentals=0)


def params(mebibytes):
    return pltpu.CompilerParams(vmem_limit_bytes=mebibytes * MIB)


def exponent_kernel(table):
    table[...] = iota(table.shape, 1).astype(F32) / -table.shape[1]


def first_kernel(dims, tokens, gain, q_weight, kv_weight, after, sums, lhs, rows):
    gy, seq_dev = dims
    inputs = tokens[...].astype(F32)
    seqs, width = inputs.shape
    mean = jnp.sum(inputs, 1, keepdims=True) / width
    centred = inputs - mean
    square = jnp.sum(centred * centred, 1, keepdims=True)
    scaled = centred * gain[...]
    each = seq_dev + 1
    for a in range(gy):
        rows[a * each : a * each + seq_dev, :] = scaled[a * seq_dev : (a + 1) * seq_dev]
        rows[a * each + seq_dev : (a + 1) * each, :] = gain[...]
    lhs[...] = rows[...].astype(BF16)

    lanes = sums.shape[1] - q_weight.shape[1] - kv_weight.shape[1]
    lane = iota((seqs, lanes), 1)
    first = iota((seqs, lanes), 0) * 6
    marks = jnp.zeros((seqs, lanes), F32)
    for place, term in enumerate(thirds(mean) + thirds(square)):
        marks = jnp.where(lane == first + place, term, marks)
    marks = jnp.broadcast_to(jnp.sum(marks, 0, keepdims=True), (gy * each, lanes))

    values = lhs[...]
    query = jnp.dot(values, q_weight[...], preferred_element_type=F32)
    keyval = jnp.dot(values, kv_weight[...], preferred_element_type=F32)
    sums[...] = jnp.concatenate([query, keyval, marks], 1).astype(BF16)


def centring(dims, parts, width):
    gx, gy, seq_dev, features = dims
    each = seq_dev + 1
    place = iota((gy * each, 1), 0)
    valid = place % each < seq_dev
    first = (place // each * seq_dev + place % each) * 6
    means, squares = [], 0.0
    for part in parts:
        marks = part[:, width:].astype(F32)
        means.append(jnp.where(valid, from_lanes(marks, first, 3), 0.0))
        squares += from_lanes(marks, first + 3, 3)
    center = sum(means) / gx
    shifts = [mean - center for mean in means]
    spread = squares / features + sum(s * s for s in shifts) / gx
    return shifts, jnp.where(valid, lax.rsqrt(spread + epsilon), 0.0)


def shifted_sum(parts, shifts, seq_dev):
    total = 0.0
    for part, shift in zip(parts, shifts):
        part = part.astype(F32)
        total += part + shift * part[seq_dev : seq_dev + 1]
    return total


def product(lhs, weight, store, slab=1024):
    for start in range(0, weight.shape[1], slab):
        part = slice(start, min(start + slab, weight.shape[1]))
        store(part, jnp.dot(lhs, weight[:, part], preferred_element_type=F32))


def gate_kernel(lhs, weight, sums):
    def store(part, value):
        sums[:, part] = value.astype(BF16)

    product(lhs[...], weight, store)


def up_kernel(lhs, weight, gate, after, both):
    rows = lhs.shape[0]
    both[:rows, :] = gate[...]

    def store(part, value):
        both[rows:, part] = value.astype(BF16)

    product(lhs[...], weight, store)


def query_kernel(dims, *refs):
    gx, gy, seq_dev, q_dev, features = dims
    parts, (query, keyval, stats) = refs[:gx], refs[gx:]
    width = q_dev + keyval.shape[1]
    shifts, inverse = centring((gx, gy, seq_dev, features), parts, width)
    for step in range(gx):
        stats[step] = jnp.broadcast_to(shifts[step], stats.shape[1:])
    stats[gx] = jnp.broadcast_to(inverse, stats.shape[1:])
    whole = shifted_sum([part[:, :width] for part in parts], shifts, seq_dev) * inverse
    query[...] = whole[:, :q_dev].astype(BF16)
    keyval[...] = whole[:, q_dev:]


def attention_kernel(dims, *refs):
    gy, gz, seq_dev = dims
    each = seq_dev + 1
    parts, refs = refs[:gy], refs[gy:]
    caches, refs = refs[:gz], refs[gz:]
    lengths, keyval, tables, after = refs[:4]
    pieces, (new_kv, qs, ks, vs) = refs[4 : 4 + gy], refs[4 + gy :]
    ctx_dev, head_dim = caches[0].shape[1], caches[0].shape[2] // 2
    heads_dev = parts[0].shape[1] // head_dim
    row = lax.axis_index("gy")

    def own_rows(values):
        mine = values[:each]
        for a in range(1, gy):
            mine = jnp.where(row == a, values[a * each : (a + 1) * each], mine)
        return mine

    cosine, sine = tables[0], tables[1]
    fresh = own_rows(keyval[...])
    fresh = jnp.concatenate(
        [rotated_halves(fresh[:, :head_dim], cosine, sine), fresh[:, head_dim:]], 1
    ).astype(BF16)
    new_kv[...] = fresh[:seq_dev]
    fresh = fresh.astype(F32)
    for da in range(gy):
        query = own_rows(parts[da][...].astype(F32))
        for h in range(heads_dev):
            start = (da * heads_dev + h) * each
            part = slice(start, start + each)
            qs[part, :] = rotated_halves(query[:, h * head_dim : (h + 1) * head_dim], cosine, sine)
            ks[part, :] = fresh[:, :head_dim]
            vs[part, :] = fresh[:, head_dim:]

    count = heads_dev * each
    many = gy * count
    scale = head_dim ** (-0.5)
    queries = qs[...].astype(BF16)
    own = jnp.sum(queries.astype(F32) * ks[...], 1, keepdims=True) * scale
    sequence = iota((many, 1), 0) % each
    scores = []
    for db in range(gz):
        block = lax.axis_index("gx") * gz + (lax.axis_index("gz") ^ db)
        positions = block * ctx_dev + iota((many, ctx_dev), 1)
        found = jnp.full((many, ctx_dev), masked_fill, F32)
        for s in range(seq_dev):
            value = lax.dot_general(
                queries,
                caches[db][s, :, :head_dim],
                (((1,), (1,)), ((), ())),
                preferred_element_type=F32,
            )
            found = jnp.where((positions < lengths[s]) & (sequence == s), value * scale, found)
        scores.append(found)
    top = own
    for found in scores:
        top = jnp.maximum(top, jnp.max(found, 1, keepdims=True))
    own_weight = jnp.where(lax.axis_index("gx") == 0, jnp.exp(own - top), 0.0)
    denom = own_weight
    numer = own_weight * vs[...]
    for db in range(gz):
        weights = jnp.where(scores[db] > 0.5 * masked_fill, jnp.exp(scores[db] - top), 0.0)
        denom += jnp.sum(weights, 1, keepdims=True)
        for s in range(seq_dev):
            mine = jnp.where(sequence == s, weights, 0.0).astype(BF16)
            numer += jnp.dot(mine, caches[db][s, :, head_dim:], preferred_element_type=F32)

    lane = iota((many, head_dim), 1)
    terms = jnp.zeros((many, head_dim), F32)
    for j, term in enumerate(thirds(top) + thirds(denom)):
        terms = jnp.where((lane == sequence * 6 + j) & (sequence < seq_dev), term, terms)
    spare = jnp.zeros((many, head_dim), F32)
    for step in range(1, each):
        spare += pltpu.roll(terms, step, 0)
    out = jnp.where(sequence == seq_dev, spare, numer)
    for da in range(gy):
        pieces[da][...] = out[da * count : (da + 1) * count].astype(BF16)


def down_kernel(dims, stats, *refs):
    gx, seq_dev = dims
    parts, (down, result, hidden) = refs[:gx], refs[gx:]
    rows, ff_dev = hidden.shape
    slab = min(ff_dev, 1024)
    inverse = stats[gx][:, :1]
    shifts = [stats[step][:, :1] for step in range(gx)]
    for start in range(0, ff_dev, slab):
        sums = []
        for base in (0, rows):
            found = [part[base : base + rows, start : start + slab] for part in parts]
            sums.append(shifted_sum(found, shifts, seq_dev) * inverse)
        gate, upward = sums
        hidden[:, start : start + slab] = (gate / (1.0 + jnp.exp(-gate)) * upward).astype(BF16)

    def store(part, value):
        result[:, part] = value

    product(hidden[...], down, store)


def out_kernel(dims, *refs):
    gx, gy, seq_dev = dims
    parts, (out_weight, partial, total, share, turned, att) = refs[:gx], refs[gx:]
    each = seq_dev + 1
    count, head_dim = parts[0].shape[1:]
    sequence = iota((count, 1), 0) % each
    valid = sequence < seq_dev
    lanes = min(128, head_dim)
    row = lax.axis_index("gy")
    for da in range(gy):
        values, tops, denoms = [], [], []
        for part in parts:
            piece = part[da].astype(F32)
            spare = jnp.where(valid, 0.0, piece[:, :lanes])
            marks = spare
            for step in range(1, each):
                marks += pltpu.roll(spare, count - step, 0)
            values.append(piece)
            tops.append(from_lanes(marks, sequence * 6, 3))
            denoms.append(from_lanes(marks, sequence * 6 + 3, 3))
        top = functools.reduce(jnp.maximum, tops)
        numer, denom = 0.0, 0.0
        for value, mine, part in zip(values, tops, denoms):
            factor = jnp.exp(mine - top)
            numer += value * factor
            denom += part * factor
        ratio = jnp.where(valid, numer / jnp.where(valid, denom, 1.0), 0.0)
        for h in range(count // each):
            turned[row ^ da, :, h * head_dim : (h + 1) * head_dim] = ratio[
                h * each : (h + 1) * each
            ]
    for a in range(gy):
        att[a * each : (a + 1) * each, :] = turned[a]
    result = partial[...] + jnp.dot(
        att[...].astype(BF16), out_weight[...], preferred_element_type=F32
    )
    for a in range(gy):
        total[a * seq_dev : (a + 1) * seq_dev, :] = result[a * each : a * each + seq_dev]
    share[...] = total[...].astype(BF16)


def with_others(values, axis):
    size = lax.axis_size(axis)
    if size <= FEW:
        return [values] + [
            lax.ppermute(values, axis, [(place, place ^ step) for place in range(size)])
            for step in range(1, size)
        ]
    gathered = lax.all_gather(values, axis)
    here = lax.axis_index(axis)
    return [lax.dynamic_index_in_dim(gathered, here ^ step, 0, False) for step in range(size)]


def body(
    tokens,
    norm_gain,
    q_weight,
    kv_weight,
    out_weight,
    gate_weight,
    up_weight,
    down_weight,
    kv_cache,
    lengths,
):
    gx, gy, gz = (lax.axis_size(axis) for axis in ("gx", "gy", "gz"))
    seqs, width = tokens.shape
    seq_dev = lengths.shape[0]
    head_dim = kv_weight.shape[1] // 2
    q_dev = q_weight.shape[1]
    ff_dev = gate_weight.shape[1]
    each = seq_dev + 1
    rows = gy * each
    count = q_dev // head_dim * each
    lanes = -(-seqs * 6 // 128) * 128

    caches = with_others(kv_cache, "gz")

    exponents = pl.pallas_call(
        exponent_kernel,
        out_shape=jax.ShapeDtypeStruct((1, head_dim // 2), F32),
        out_specs=VMEM,
        compiler_params=params(LIMIT),
        cost_estimate=cost(7e9, 0),
        name="exponents",
    )()
    sums, lhs = pl.pallas_call(
        functools.partial(first_kernel, (gy, seq_dev)),
        out_shape=(
            jax.ShapeDtypeStruct((rows, q_dev + 2 * head_dim + lanes), BF16),
            jax.ShapeDtypeStruct((rows, width), BF16),
        ),
        in_specs=[VMEM] * 4 + [ANY],
        out_specs=(VMEM, VMEM),
        scratch_shapes=[pltpu.VMEM((rows, width), F32)],
        compiler_params=params(LIMIT),
        cost_estimate=cost(7e9, 0),
        name="norm_query",
    )(tokens, norm_gain[None, :], q_weight, kv_weight, exponents)
    sums = with_others(sums, "gx")

    gate = pl.pallas_call(
        gate_kernel,
        out_shape=jax.ShapeDtypeStruct((rows, ff_dev), BF16),
        in_specs=[VMEM, VMEM],
        out_specs=VMEM,
        compiler_params=params(LIMIT),
        cost_estimate=cost(6e9, 16.8e6),
        name="gate",
    )(lhs, gate_weight)
    query, keyval, stats = pl.pallas_call(
        functools.partial(query_kernel, (gx, gy, seq_dev, q_dev, gx * width)),
        out_shape=(
            jax.ShapeDtypeStruct((rows, q_dev), BF16),
            jax.ShapeDtypeStruct((rows, 2 * head_dim), F32),
            jax.ShapeDtypeStruct((gx + 1, rows, 128), F32),
        ),
        in_specs=[VMEM] * gx,
        out_specs=(VMEM,) * 3,
        compiler_params=params(LIMIT),
        cost_estimate=cost(1e8, 1e5),
        name="query_sum",
    )(*sums)
    queries = with_others(query, "gy")
    both = pl.pallas_call(
        up_kernel,
        out_shape=jax.ShapeDtypeStruct((2 * rows, ff_dev), BF16),
        in_specs=[VMEM] * 3 + [ANY],
        out_specs=VMEM,
        compiler_params=params(LIMIT),
        cost_estimate=cost(6e9, 16.8e6),
        name="up",
    )(lhs, up_weight, gate, query)
    parts = with_others(both, "gx")

    angle = lengths.astype(F32)[:, None] * rotary_base**exponents
    angle = jnp.pad(angle, ((0, 1), (0, 0)))
    tables = jnp.stack([jnp.cos(angle), jnp.sin(angle)])
    *pieces, new_kv = pl.pallas_call(
        functools.partial(attention_kernel, (gy, gz, seq_dev)),
        out_shape=(jax.ShapeDtypeStruct((count, head_dim), BF16),) * gy
        + (jax.ShapeDtypeStruct((seq_dev, 2 * head_dim), BF16),),
        in_specs=[VMEM] * (gz + gy) + [SMEM, VMEM, VMEM, ANY],
        out_specs=(VMEM,) * (gy + 1),
        scratch_shapes=[pltpu.VMEM((gy * count, head_dim), F32)] * 3,
        compiler_params=params(LIMIT),
        cost_estimate=cost(7e9, 2e6),
        name="attention",
    )(*queries, *caches, lengths, keyval, tables, both)
    pieces = pieces[:1] + [
        lax.ppermute(pieces[step], "gy", [(place, place ^ step) for place in range(gy)])
        for step in range(1, gy)
    ]
    pieces = with_others(jnp.stack(pieces), "gx")

    partial = pl.pallas_call(
        functools.partial(down_kernel, (gx, seq_dev)),
        out_shape=jax.ShapeDtypeStruct((rows, width), F32),
        in_specs=[VMEM] * (gx + 2),
        out_specs=VMEM,
        scratch_shapes=[pltpu.VMEM((rows, ff_dev), BF16)],
        compiler_params=params(LIMIT),
        cost_estimate=cost(4e9, 16.8e6),
        name="hidden_down",
    )(stats, *parts, down_weight)
    total, share = pl.pallas_call(
        functools.partial(out_kernel, (gx, gy, seq_dev)),
        out_shape=(
            jax.ShapeDtypeStruct((seqs, width), F32),
            jax.ShapeDtypeStruct((seqs, width), BF16),
        ),
        in_specs=[VMEM] * (gx + 2),
        out_specs=(VMEM, VMEM),
        scratch_shapes=[pltpu.VMEM((gy, each, q_dev), F32), pltpu.VMEM((rows, q_dev), F32)],
        compiler_params=params(LIMIT if gx <= FEW else 4 * LIMIT),
        cost_estimate=cost(1e9, 4e6),
        name="out_projection",
    )(*pieces, out_weight, partial)
    for other in with_others(share, ("gy", "gz"))[1:]:
        total = total + other.astype(F32)
    mixed = (tokens.astype(F32) + total).astype(BF16)
    return (mixed, new_kv)


def solution(mesh):
    in_specs = (
        P("group", "gx"),
        P("gx"),
        P("gx", ("gy", "gz")),
        P("gx", None),
        P(("gy", "gz"), "gx"),
        P("gx", ("gy", "gz")),
        P("gx", ("gy", "gz")),
        P(("gy", "gz"), "gx"),
        P(("group", "gy"), ("gx", "gz"), None),
        P(("group", "gy")),
    )
    out_specs = (P("group", "gx"), P(("group", "gy"), None))
    return jax.shard_map(body, mesh=mesh, in_specs=in_specs, out_specs=out_specs, check_vma=False)
```

```python
import functools

import jax
import jax.numpy as jnp
from jax import lax
from jax.experimental import pallas as pl
from jax.experimental.pallas import tpu as pltpu
from jax.sharding import PartitionSpec as P

epsilon = 1e-05
masked_fill = -1e30
rotary_base = 10000.0
FEW = 8
LIMIT = 3
F32 = jnp.float32
BF16 = jnp.bfloat16
VMEM = pl.BlockSpec(memory_space=pltpu.VMEM)
SMEM = pl.BlockSpec(memory_space=pltpu.SMEM)
ANY = pl.BlockSpec(memory_space=pl.ANY)
HBM = pl.BlockSpec(memory_space=pltpu.HBM)
MIB = 2**20


def iota(shape, dim):
    return lax.broadcasted_iota(jnp.int32, shape, dim)


def thirds(values):
    high = values.astype(BF16).astype(F32)
    rest = values - high
    middle = rest.astype(BF16).astype(F32)
    return high, middle, rest - middle


def from_lanes(row, first, count):
    lane = iota(row.shape, 1)
    return jnp.sum(jnp.where((lane >= first) & (lane < first + count), row, 0.0), 1, keepdims=True)


def rotated_halves(values, cosine, sine):
    middle = values.shape[-1] // 2
    first, second = values[:, :middle], values[:, middle:]
    return jnp.concatenate(
        [first * cosine - second * sine, first * sine + second * cosine], 1
    )


def cost(flops, nbytes):
    return pl.CostEstimate(flops=int(flops), bytes_accessed=int(nbytes), transcendentals=0)


def params(mebibytes):
    return pltpu.CompilerParams(vmem_limit_bytes=mebibytes * MIB)


def exponent_kernel(table):
    table[...] = iota(table.shape, 1).astype(F32) / -table.shape[1]


def first_kernel(dims, tokens, gain, q_weight, kv_weight, after, sums, lhs, rows):
    gy, seq_dev = dims
    inputs = tokens[...].astype(F32)
    seqs, width = inputs.shape
    mean = jnp.sum(inputs, 1, keepdims=True) / width
    centred = inputs - mean
    square = jnp.sum(centred * centred, 1, keepdims=True)
    scaled = centred * gain[...]
    each = seq_dev + 1
    for a in range(gy):
        rows[a * each : a * each + seq_dev, :] = scaled[a * seq_dev : (a + 1) * seq_dev]
        rows[a * each + seq_dev : (a + 1) * each, :] = gain[...]
    lhs[...] = rows[...].astype(BF16)

    lanes = sums.shape[1] - q_weight.shape[1] - kv_weight.shape[1]
    lane = iota((seqs, lanes), 1)
    first = iota((seqs, lanes), 0) * 6
    marks = jnp.zeros((seqs, lanes), F32)
    for place, term in enumerate(thirds(mean) + thirds(square)):
        marks = jnp.where(lane == first + place, term, marks)
    marks = jnp.broadcast_to(jnp.sum(marks, 0, keepdims=True), (gy * each, lanes))

    values = lhs[...]
    query = jnp.dot(values, q_weight[...], preferred_element_type=F32)
    keyval = jnp.dot(values, kv_weight[...], preferred_element_type=F32)
    sums[...] = jnp.concatenate([query, keyval, marks], 1).astype(BF16)


def centring(dims, parts, width):
    gx, gy, seq_dev, features = dims
    each = seq_dev + 1
    place = iota((gy * each, 1), 0)
    valid = place % each < seq_dev
    first = (place // each * seq_dev + place % each) * 6
    means, squares = [], 0.0
    for part in parts:
        marks = part[:, width:].astype(F32)
        means.append(jnp.where(valid, from_lanes(marks, first, 3), 0.0))
        squares += from_lanes(marks, first + 3, 3)
    center = sum(means) / gx
    shifts = [mean - center for mean in means]
    spread = squares / features + sum(s * s for s in shifts) / gx
    return shifts, jnp.where(valid, lax.rsqrt(spread + epsilon), 0.0)


def shifted_sum(parts, shifts, seq_dev):
    total = 0.0
    for part, shift in zip(parts, shifts):
        part = part.astype(F32)
        total += part + shift * part[seq_dev : seq_dev + 1]
    return total


def product(lhs, weight, store, slab=1024):
    for start in range(0, weight.shape[1], slab):
        part = slice(start, min(start + slab, weight.shape[1]))
        store(part, jnp.dot(lhs, weight[:, part], preferred_element_type=F32))


def gate_kernel(lhs, weight, sums):
    def store(part, value):
        sums[:, part] = value.astype(BF16)

    product(lhs[...], weight, store)


def up_kernel(lhs, weight, gate, after, both):
    rows = lhs.shape[0]
    both[:rows, :] = gate[...]

    def store(part, value):
        both[rows:, part] = value.astype(BF16)

    product(lhs[...], weight, store)


def query_kernel(dims, *refs):
    gx, gy, seq_dev, q_dev, features = dims
    parts, (query, keyval, stats) = refs[:gx], refs[gx:]
    width = q_dev + keyval.shape[1]
    shifts, inverse = centring((gx, gy, seq_dev, features), parts, width)
    for step in range(gx):
        stats[step] = jnp.broadcast_to(shifts[step], stats.shape[1:])
    stats[gx] = jnp.broadcast_to(inverse, stats.shape[1:])
    whole = shifted_sum([part[:, :width] for part in parts], shifts, seq_dev) * inverse
    query[...] = whole[:, :q_dev].astype(BF16)
    keyval[...] = whole[:, q_dev:]


def attention_kernel(dims, *refs):
    gy, gz, seq_dev = dims
    each = seq_dev + 1
    parts, refs = refs[:gy], refs[gy:]
    caches, refs = refs[:gz], refs[gz:]
    lengths, keyval, tables, after = refs[:4]
    pieces, (new_kv, qs, ks, vs) = refs[4 : 4 + gy], refs[4 + gy :]
    ctx_dev, head_dim = caches[0].shape[1], caches[0].shape[2] // 2
    heads_dev = parts[0].shape[1] // head_dim
    row = lax.axis_index("gy")

    def own_rows(values):
        mine = values[:each]
        for a in range(1, gy):
            mine = jnp.where(row == a, values[a * each : (a + 1) * each], mine)
        return mine

    cosine, sine = tables[0], tables[1]
    fresh = own_rows(keyval[...])
    fresh = jnp.concatenate(
        [rotated_halves(fresh[:, :head_dim], cosine, sine), fresh[:, head_dim:]], 1
    ).astype(BF16)
    new_kv[...] = fresh[:seq_dev]
    fresh = fresh.astype(F32)
    for da in range(gy):
        query = own_rows(parts[da][...].astype(F32))
        for h in range(heads_dev):
            start = (da * heads_dev + h) * each
            part = slice(start, start + each)
            qs[part, :] = rotated_halves(query[:, h * head_dim : (h + 1) * head_dim], cosine, sine)
            ks[part, :] = fresh[:, :head_dim]
            vs[part, :] = fresh[:, head_dim:]

    count = heads_dev * each
    many = gy * count
    scale = head_dim ** (-0.5)
    queries = qs[...].astype(BF16)
    own = jnp.sum(queries.astype(F32) * ks[...], 1, keepdims=True) * scale
    sequence = iota((many, 1), 0) % each
    scores = []
    for db in range(gz):
        block = lax.axis_index("gx") * gz + (lax.axis_index("gz") ^ db)
        positions = block * ctx_dev + iota((many, ctx_dev), 1)
        found = jnp.full((many, ctx_dev), masked_fill, F32)
        for s in range(seq_dev):
            value = lax.dot_general(
                queries,
                caches[db][s, :, :head_dim],
                (((1,), (1,)), ((), ())),
                preferred_element_type=F32,
            )
            found = jnp.where((positions < lengths[s]) & (sequence == s), value * scale, found)
        scores.append(found)
    top = own
    for found in scores:
        top = jnp.maximum(top, jnp.max(found, 1, keepdims=True))
    own_weight = jnp.where(lax.axis_index("gx") == 0, jnp.exp(own - top), 0.0)
    denom = own_weight
    numer = own_weight * vs[...]
    for db in range(gz):
        weights = jnp.where(scores[db] > 0.5 * masked_fill, jnp.exp(scores[db] - top), 0.0)
        denom += jnp.sum(weights, 1, keepdims=True)
        for s in range(seq_dev):
            mine = jnp.where(sequence == s, weights, 0.0).astype(BF16)
            numer += jnp.dot(mine, caches[db][s, :, head_dim:], preferred_element_type=F32)

    lane = iota((many, head_dim), 1)
    terms = jnp.zeros((many, head_dim), F32)
    for j, term in enumerate(thirds(top) + thirds(denom)):
        terms = jnp.where((lane == sequence * 6 + j) & (sequence < seq_dev), term, terms)
    spare = jnp.zeros((many, head_dim), F32)
    for step in range(1, each):
        spare += pltpu.roll(terms, step, 0)
    out = jnp.where(sequence == seq_dev, spare, numer)
    for da in range(gy):
        pieces[da][...] = out[da * count : (da + 1) * count].astype(BF16)


def down_kernel(dims, stats, *refs):
    gx, seq_dev, order = dims
    parts, (down, result, hidden) = refs[:gx], refs[gx:]
    rows, ff_dev = hidden.shape
    slab = min(ff_dev, 1024)
    inverse = stats[gx][:, :1]
    shifts = [stats[step][:, :1] for step in (0, *order)]
    for start in range(0, ff_dev, slab):
        sums = []
        for base in (0, rows):
            found = [part[base : base + rows, start : start + slab] for part in parts]
            sums.append(shifted_sum(found, shifts, seq_dev) * inverse)
        gate, upward = sums
        hidden[:, start : start + slab] = (gate / (1.0 + jnp.exp(-gate)) * upward).astype(BF16)

    def store(part, value):
        result[:, part] = value

    product(hidden[...], down, store)


def out_kernel(dims, *refs):
    gx, gy, seq_dev = dims
    parts, (out_weight, partial, total, share, turned, att) = refs[:gx], refs[gx:]
    each = seq_dev + 1
    count, head_dim = parts[0].shape[1:]
    sequence = iota((count, 1), 0) % each
    valid = sequence < seq_dev
    lanes = min(128, head_dim)
    row = lax.axis_index("gy")
    for da in range(gy):
        values, tops, denoms = [], [], []
        for part in parts:
            piece = part[da].astype(F32)
            spare = jnp.where(valid, 0.0, piece[:, :lanes])
            marks = spare
            for step in range(1, each):
                marks += pltpu.roll(spare, count - step, 0)
            values.append(piece)
            tops.append(from_lanes(marks, sequence * 6, 3))
            denoms.append(from_lanes(marks, sequence * 6 + 3, 3))
        top = functools.reduce(jnp.maximum, tops)
        numer, denom = 0.0, 0.0
        for value, mine, part in zip(values, tops, denoms):
            factor = jnp.exp(mine - top)
            numer += value * factor
            denom += part * factor
        ratio = jnp.where(valid, numer / jnp.where(valid, denom, 1.0), 0.0)
        for h in range(count // each):
            turned[row ^ da, :, h * head_dim : (h + 1) * head_dim] = ratio[
                h * each : (h + 1) * each
            ]
    for a in range(gy):
        att[a * each : (a + 1) * each, :] = turned[a]
    result = partial[...] + jnp.dot(
        att[...].astype(BF16), out_weight[...], preferred_element_type=F32
    )
    for a in range(gy):
        total[a * seq_dev : (a + 1) * seq_dev, :] = result[a * each : a * each + seq_dev]
    share[...] = total[...].astype(BF16)


def with_others(values, axis, order=None):
    size = lax.axis_size(axis)
    if size <= FEW:
        return [values] + [
            lax.ppermute(values, axis, [(place, place ^ step) for place in range(size)])
            for step in (order or range(1, size))
        ]
    gathered = lax.all_gather(values, axis)
    here = lax.axis_index(axis)
    return [
        lax.dynamic_index_in_dim(gathered, here ^ step, 0, False)
        for step in (0, *(order or range(1, size)))
    ]


def body(
    tokens,
    norm_gain,
    q_weight,
    kv_weight,
    out_weight,
    gate_weight,
    up_weight,
    down_weight,
    kv_cache,
    lengths,
):
    gx, gy, gz = (lax.axis_size(axis) for axis in ("gx", "gy", "gz"))
    seqs, width = tokens.shape
    seq_dev = lengths.shape[0]
    head_dim = kv_weight.shape[1] // 2
    q_dev = q_weight.shape[1]
    ff_dev = gate_weight.shape[1]
    each = seq_dev + 1
    rows = gy * each
    count = q_dev // head_dim * each
    lanes = -(-seqs * 6 // 128) * 128

    caches = with_others(kv_cache, "gz")

    exponents = pl.pallas_call(
        exponent_kernel,
        out_shape=jax.ShapeDtypeStruct((1, head_dim // 2), F32),
        out_specs=VMEM,
        compiler_params=params(LIMIT),
        cost_estimate=cost(7e9, 0),
        name="exponents",
    )()
    sums, lhs = pl.pallas_call(
        functools.partial(first_kernel, (gy, seq_dev)),
        out_shape=(
            jax.ShapeDtypeStruct((rows, q_dev + 2 * head_dim + lanes), BF16),
            jax.ShapeDtypeStruct((rows, width), BF16),
        ),
        in_specs=[VMEM] * 4 + [ANY],
        out_specs=(VMEM, VMEM),
        scratch_shapes=[pltpu.VMEM((rows, width), F32)],
        compiler_params=params(LIMIT),
        cost_estimate=cost(7e9, 0),
        name="norm_query",
    )(tokens, norm_gain[None, :], q_weight, kv_weight, exponents)
    sums = with_others(sums, "gx")

    gate = pl.pallas_call(
        gate_kernel,
        out_shape=jax.ShapeDtypeStruct((rows, ff_dev), BF16),
        in_specs=[VMEM, VMEM],
        out_specs=VMEM,
        compiler_params=params(LIMIT),
        cost_estimate=cost(6e9, 16.8e6),
        name="gate",
    )(lhs, gate_weight)
    query, keyval, stats = pl.pallas_call(
        functools.partial(query_kernel, (gx, gy, seq_dev, q_dev, gx * width)),
        out_shape=(
            jax.ShapeDtypeStruct((rows, q_dev), BF16),
            jax.ShapeDtypeStruct((rows, 2 * head_dim), F32),
            jax.ShapeDtypeStruct((gx + 1, rows, 128), F32),
        ),
        in_specs=[VMEM] * gx,
        out_specs=(VMEM,) * 3,
        compiler_params=params(LIMIT),
        cost_estimate=cost(1e8, 1e5),
        name="query_sum",
    )(*sums)
    queries = with_others(query, "gy")
    both = pl.pallas_call(
        up_kernel,
        out_shape=jax.ShapeDtypeStruct((2 * rows, ff_dev), BF16),
        in_specs=[VMEM] * 3 + [ANY],
        out_specs=VMEM,
        compiler_params=params(LIMIT),
        cost_estimate=cost(6e9, 16.8e6),
        name="up",
    )(lhs, up_weight, gate, query)
    order = (1, 3, 2) if gx == 4 else tuple(range(1, gx))
    parts = with_others(both, "gx", order)

    angle = lengths.astype(F32)[:, None] * rotary_base**exponents
    angle = jnp.pad(angle, ((0, 1), (0, 0)))
    tables = jnp.stack([jnp.cos(angle), jnp.sin(angle)])
    *pieces, new_kv = pl.pallas_call(
        functools.partial(attention_kernel, (gy, gz, seq_dev)),
        out_shape=(jax.ShapeDtypeStruct((count, head_dim), BF16),) * gy
        + (jax.ShapeDtypeStruct((seq_dev, 2 * head_dim), BF16),),
        in_specs=[VMEM] * (gz + gy) + [SMEM, VMEM, VMEM, ANY],
        out_specs=(VMEM,) * (gy + 1),
        scratch_shapes=[pltpu.VMEM((gy * count, head_dim), F32)] * 3,
        compiler_params=params(LIMIT),
        cost_estimate=cost(7e9, 2e6),
        name="attention",
    )(*queries, *caches, lengths, keyval, tables, both)
    pieces = pieces[:1] + [
        lax.ppermute(pieces[step], "gy", [(place, place ^ step) for place in range(gy)])
        for step in range(1, gy)
    ]
    pieces = with_others(jnp.stack(pieces), "gx")

    partial = pl.pallas_call(
        functools.partial(down_kernel, (gx, seq_dev, order)),
        out_shape=jax.ShapeDtypeStruct((rows, width), F32),
        in_specs=[VMEM] * (gx + 2),
        out_specs=VMEM,
        scratch_shapes=[pltpu.VMEM((rows, ff_dev), BF16)],
        compiler_params=params(LIMIT),
        cost_estimate=cost(4e9, 16.8e6),
        name="hidden_down",
    )(stats, *parts, down_weight)
    total, share = pl.pallas_call(
        functools.partial(out_kernel, (gx, gy, seq_dev)),
        out_shape=(
            jax.ShapeDtypeStruct((seqs, width), F32),
            jax.ShapeDtypeStruct((seqs, width), BF16),
        ),
        in_specs=[VMEM] * (gx + 2),
        out_specs=(VMEM, VMEM),
        scratch_shapes=[pltpu.VMEM((gy, each, q_dev), F32), pltpu.VMEM((rows, q_dev), F32)],
        compiler_params=params(LIMIT if gx <= FEW else 4 * LIMIT),
        cost_estimate=cost(1e9, 4e6),
        name="out_projection",
    )(*pieces, out_weight, partial)
    for other in with_others(share, ("gy", "gz"))[1:]:
        total = total + other.astype(F32)
    mixed = (tokens.astype(F32) + total).astype(BF16)
    return (mixed, new_kv)


def solution(mesh):
    in_specs = (
        P("group", "gx"),
        P("gx"),
        P("gx", ("gy", "gz")),
        P("gx", None),
        P(("gy", "gz"), "gx"),
        P("gx", ("gy", "gz")),
        P("gx", ("gy", "gz")),
        P(("gy", "gz"), "gx"),
        P(("group", "gy"), ("gx", "gz"), None),
        P(("group", "gy")),
    )
    out_specs = (P("group", "gx"), P(("group", "gy"), None))
    return jax.shard_map(body, mesh=mesh, in_specs=in_specs, out_specs=out_specs, check_vma=False)
```

```python
import functools

import jax
import jax.numpy as jnp
from jax import lax
from jax.experimental import pallas as pl
from jax.experimental.pallas import tpu as pltpu
from jax.sharding import PartitionSpec as P

epsilon = 1e-05
masked_fill = -1e30
rotary_base = 10000.0
FEW = 8
LIMIT = 3
SPARE = 512
F32 = jnp.float32
BF16 = jnp.bfloat16
VMEM = pl.BlockSpec(memory_space=pltpu.VMEM)
ANY = pl.BlockSpec(memory_space=pl.ANY)
HBM = pl.BlockSpec(memory_space=pltpu.HBM)
MIB = 2**20


def iota(shape, dim):
    return lax.broadcasted_iota(jnp.int32, shape, dim)


def thirds(values):
    high = values.astype(BF16).astype(F32)
    rest = values - high
    middle = rest.astype(BF16).astype(F32)
    return high, middle, rest - middle


def from_lanes(row, first, count):
    lane = iota(row.shape, 1)
    return jnp.sum(jnp.where((lane >= first) & (lane < first + count), row, 0.0), 1, keepdims=True)


def rotated_halves(values, cosine, sine):
    middle = values.shape[-1] // 2
    first, second = values[:, :middle], values[:, middle:]
    return jnp.concatenate(
        [first * cosine - second * sine, first * sine + second * cosine], 1
    )


def cost(flops, nbytes):
    return pl.CostEstimate(flops=int(flops), bytes_accessed=int(nbytes), transcendentals=0)


def params(mebibytes):
    return pltpu.CompilerParams(vmem_limit_bytes=mebibytes * MIB)


def exponent_kernel(table):
    table[...] = iota(table.shape, 1).astype(F32) / -table.shape[1]


def first_kernel(dims, tokens, gain, q_weight, kv_weight, after, sums, lhs, rows):
    gy, seq_dev = dims
    inputs = tokens[...].astype(F32)
    seqs, width = inputs.shape
    mean = jnp.sum(inputs, 1, keepdims=True) / width
    centred = inputs - mean
    square = jnp.sum(centred * centred, 1, keepdims=True)
    scaled = centred * gain[...]
    each = seq_dev + 1
    for a in range(gy):
        rows[a * each : a * each + seq_dev, :] = scaled[a * seq_dev : (a + 1) * seq_dev]
        rows[a * each + seq_dev : (a + 1) * each, :] = gain[...]
    lhs[...] = rows[...].astype(BF16)

    lanes = sums.shape[1] - q_weight.shape[1] - kv_weight.shape[1]
    lane = iota((seqs, lanes), 1)
    first = iota((seqs, lanes), 0) * 6
    marks = jnp.zeros((seqs, lanes), F32)
    for place, term in enumerate(thirds(mean) + thirds(square)):
        marks = jnp.where(lane == first + place, term, marks)
    marks = jnp.broadcast_to(jnp.sum(marks, 0, keepdims=True), (gy * each, lanes))

    values = lhs[...]
    query = jnp.dot(values, q_weight[...], preferred_element_type=F32)
    keyval = jnp.dot(values, kv_weight[...], preferred_element_type=F32)
    sums[...] = jnp.concatenate([query, keyval, marks], 1).astype(BF16)


def centring(dims, parts, width):
    gx, gy, seq_dev, features = dims
    each = seq_dev + 1
    place = iota((gy * each, 1), 0)
    valid = place % each < seq_dev
    first = (place // each * seq_dev + place % each) * 6
    means, squares = [], 0.0
    for part in parts:
        marks = part[:, width:].astype(F32)
        means.append(jnp.where(valid, from_lanes(marks, first, 3), 0.0))
        squares += from_lanes(marks, first + 3, 3)
    center = sum(means) / gx
    shifts = [mean - center for mean in means]
    spread = squares / features + sum(s * s for s in shifts) / gx
    return shifts, jnp.where(valid, lax.rsqrt(spread + epsilon), 0.0)


def shifted_sum(parts, shifts, seq_dev):
    total = 0.0
    for part, shift in zip(parts, shifts):
        part = part.astype(F32)
        total += part + shift * part[seq_dev : seq_dev + 1]
    return total


def product(lhs, weight, store, slab=1024):
    for start in range(0, weight.shape[1], slab):
        part = slice(start, min(start + slab, weight.shape[1]))
        store(part, jnp.dot(lhs, weight[:, part], preferred_element_type=F32))


def gate_kernel(lhs, weight, sums):
    def store(part, value):
        sums[:, part] = value.astype(BF16)

    product(lhs[...], weight, store)


def packed_split(rows, each, ff_dev):
    slab = ff_dev // rows * 2
    if rows == 2 * each and (rows - 1) * slab == 2 * ff_dev - slab and slab % 128 == 0:
        return ff_dev - slab
    return ff_dev


def up_kernel(lhs, weight, gate, after, both, wide):
    rows, ff_dev = gate.shape
    stay = wide.shape[1] - ff_dev
    wide[:, :ff_dev] = gate[...].astype(F32)

    def store(part, value):
        if part.start < stay:
            wide[:, ff_dev + part.start : ff_dev + part.stop] = value
        else:
            size = part.stop - part.start
            for r in range(rows - 1):
                wide[rows - 1 :, r * size : (r + 1) * size] = value[r : r + 1]

    product(lhs[...], weight, store, ff_dev - stay or 1024)
    both[:, : wide.shape[1]] = wide[...].astype(BF16)
    both[:, wide.shape[1] :] = jnp.zeros_like(both[:, wide.shape[1] :])


def query_kernel(dims, *refs):
    gx, gy, seq_dev, q_dev, features = dims
    parts, (query, keyval, stats) = refs[:gx], refs[gx:]
    width = q_dev + keyval.shape[1]
    shifts, inverse = centring((gx, gy, seq_dev, features), parts, width)
    for step in range(gx):
        stats[step] = jnp.broadcast_to(shifts[step], stats.shape[1:])
    stats[gx] = jnp.broadcast_to(inverse, stats.shape[1:])
    whole = shifted_sum([part[:, :width] for part in parts], shifts, seq_dev) * inverse
    query[...] = whole[:, :q_dev].astype(BF16)
    keyval[...] = whole[:, q_dev:]


def attention_kernel(dims, *refs):
    gy, gz, seq_dev = dims
    each = seq_dev + 1
    parts, refs = refs[:gy], refs[gy:]
    caches, refs = refs[:gz], refs[gz:]
    keyval, tables, after = refs[:3]
    pieces, (new_kv, qs, ks, vs) = refs[3 : 3 + gy], refs[3 + gy :]
    ctx_dev, head_dim = caches[0].shape[1], caches[0].shape[2] // 2
    heads_dev = parts[0].shape[1] // head_dim
    row = lax.axis_index("gy")

    def own_rows(values):
        mine = values[:each]
        for a in range(1, gy):
            mine = jnp.where(row == a, values[a * each : (a + 1) * each], mine)
        return mine

    cosine, sine, lengths = tables[0], tables[1], tables[2]
    fresh = own_rows(keyval[...])
    fresh = jnp.concatenate(
        [rotated_halves(fresh[:, :head_dim], cosine, sine), fresh[:, head_dim:]], 1
    ).astype(BF16)
    new_kv[...] = fresh[:seq_dev]
    fresh = fresh.astype(F32)
    for da in range(gy):
        query = own_rows(parts[da][...].astype(F32))
        for h in range(heads_dev):
            start = (da * heads_dev + h) * each
            part = slice(start, start + each)
            qs[part, :] = rotated_halves(query[:, h * head_dim : (h + 1) * head_dim], cosine, sine)
            ks[part, :] = fresh[:, :head_dim]
            vs[part, :] = fresh[:, head_dim:]

    count = heads_dev * each
    many = gy * count
    scale = head_dim ** (-0.5)
    queries = qs[...].astype(BF16)
    own = jnp.sum(queries.astype(F32) * ks[...], 1, keepdims=True) * scale
    sequence = iota((many, 1), 0) % each
    scores = []
    for db in range(gz):
        block = lax.axis_index("gx") * gz + (lax.axis_index("gz") ^ db)
        positions = (block * ctx_dev + iota((many, ctx_dev), 1)).astype(F32)
        found = jnp.full((many, ctx_dev), masked_fill, F32)
        for s in range(seq_dev):
            value = lax.dot_general(
                queries,
                caches[db][s, :, :head_dim],
                (((1,), (1,)), ((), ())),
                preferred_element_type=F32,
            )
            found = jnp.where((positions < lengths[s : s + 1, :1]) & (sequence == s), value * scale, found)
        scores.append(found)
    top = own
    for found in scores:
        top = jnp.maximum(top, jnp.max(found, 1, keepdims=True))
    own_weight = jnp.where(lax.axis_index("gx") == 0, jnp.exp(own - top), 0.0)
    denom = own_weight
    numer = own_weight * vs[...]
    for db in range(gz):
        weights = jnp.where(scores[db] > 0.5 * masked_fill, jnp.exp(scores[db] - top), 0.0)
        denom += jnp.sum(weights, 1, keepdims=True)
        for s in range(seq_dev):
            mine = jnp.where(sequence == s, weights, 0.0).astype(BF16)
            numer += jnp.dot(mine, caches[db][s, :, head_dim:], preferred_element_type=F32)

    lane = iota((many, head_dim), 1)
    terms = jnp.zeros((many, head_dim), F32)
    for j, term in enumerate(thirds(top) + thirds(denom)):
        terms = jnp.where((lane == sequence * 6 + j) & (sequence < seq_dev), term, terms)
    spare = jnp.zeros((many, head_dim), F32)
    for step in range(1, each):
        spare += pltpu.roll(terms, step, 0)
    out = jnp.where(sequence == seq_dev, spare, numer)
    for da in range(gy):
        pieces[da][...] = out[da * count : (da + 1) * count].astype(BF16)


def down_kernel(dims, stats, *refs):
    gx, seq_dev, order = dims
    parts, (down, result, hidden, left) = refs[:gx], refs[gx:]
    rows, ff_dev = hidden.shape
    stay = parts[0].shape[1] - ff_dev - SPARE
    slab = ff_dev - stay or min(ff_dev, 1024)
    inverse = stats[gx][:, :1]
    shifts = [stats[step][:, :1] for step in (0, *order)]

    def summed(start):
        found = [part[:, start : start + slab] for part in parts]
        return shifted_sum(found, shifts, seq_dev)

    if stay < ff_dev:
        left[...] = jnp.zeros_like(left)
        blocks = [
            [part[:, r * slab : (r + 1) * slab].astype(F32)[rows - 1 :] for r in range(rows - 1)]
            for part in parts
        ]
        for r in range(rows - 1):
            left[r : r + 1, :] = sum(
                block[r] + shift[r : r + 1] * block[seq_dev] for block, shift in zip(blocks, shifts)
            )
    for start in range(0, ff_dev, slab):
        gate = summed(start) * inverse
        upward = (summed(ff_dev + start) if start < stay else left[...]) * inverse
        hidden[:, start : start + slab] = (gate / (1.0 + jnp.exp(-gate)) * upward).astype(BF16)

    def store(part, value):
        result[:, part] = value

    product(hidden[...], down, store)


def out_kernel(dims, *refs):
    gx, gy, seq_dev = dims
    parts, (out_weight, partial, total, share, turned, att) = refs[:gx], refs[gx:]
    each = seq_dev + 1
    count, head_dim = parts[0].shape[1:]
    sequence = iota((count, 1), 0) % each
    valid = sequence < seq_dev
    lanes = min(128, head_dim)
    row = lax.axis_index("gy")
    for da in range(gy):
        values, tops, denoms = [], [], []
        for part in parts:
            piece = part[da].astype(F32)
            spare = jnp.where(valid, 0.0, piece[:, :lanes])
            marks = spare
            for step in range(1, each):
                marks += pltpu.roll(spare, count - step, 0)
            values.append(piece)
            tops.append(from_lanes(marks, sequence * 6, 3))
            denoms.append(from_lanes(marks, sequence * 6 + 3, 3))
        top = functools.reduce(jnp.maximum, tops)
        numer, denom = 0.0, 0.0
        for value, mine, part in zip(values, tops, denoms):
            factor = jnp.exp(mine - top)
            numer += value * factor
            denom += part * factor
        ratio = jnp.where(valid, numer / jnp.where(valid, denom, 1.0), 0.0)
        for h in range(count // each):
            turned[row ^ da, :, h * head_dim : (h + 1) * head_dim] = ratio[
                h * each : (h + 1) * each
            ]
    for a in range(gy):
        att[a * each : (a + 1) * each, :] = turned[a]
    result = partial[...] + jnp.dot(
        att[...].astype(BF16), out_weight[...], preferred_element_type=F32
    )
    for a in range(gy):
        total[a * seq_dev : (a + 1) * seq_dev, :] = result[a * each : a * each + seq_dev]
    share[...] = total[...].astype(BF16)


def with_others(values, axis, order=None):
    size = lax.axis_size(axis)
    if size <= FEW:
        return [values] + [
            lax.ppermute(values, axis, [(place, place ^ step) for place in range(size)])
            for step in (order or range(1, size))
        ]
    gathered = lax.all_gather(values, axis)
    here = lax.axis_index(axis)
    return [
        lax.dynamic_index_in_dim(gathered, here ^ step, 0, False)
        for step in (0, *(order or range(1, size)))
    ]


def body(
    tokens,
    norm_gain,
    q_weight,
    kv_weight,
    out_weight,
    gate_weight,
    up_weight,
    down_weight,
    kv_cache,
    lengths,
):
    gx, gy, gz = (lax.axis_size(axis) for axis in ("gx", "gy", "gz"))
    seqs, width = tokens.shape
    seq_dev = lengths.shape[0]
    head_dim = kv_weight.shape[1] // 2
    q_dev = q_weight.shape[1]
    ff_dev = gate_weight.shape[1]
    each = seq_dev + 1
    rows = gy * each
    count = q_dev // head_dim * each
    lanes = -(-seqs * 6 // 128) * 128

    caches = with_others(kv_cache, "gz")

    exponents = pl.pallas_call(
        exponent_kernel,
        out_shape=jax.ShapeDtypeStruct((1, head_dim // 2), F32),
        out_specs=VMEM,
        compiler_params=params(LIMIT),
        cost_estimate=cost(7e9, 0),
        name="exponents",
    )()
    sums, lhs = pl.pallas_call(
        functools.partial(first_kernel, (gy, seq_dev)),
        out_shape=(
            jax.ShapeDtypeStruct((rows, q_dev + 2 * head_dim + lanes), BF16),
            jax.ShapeDtypeStruct((rows, width), BF16),
        ),
        in_specs=[VMEM] * 4 + [ANY],
        out_specs=(VMEM, VMEM),
        scratch_shapes=[pltpu.VMEM((rows, width), F32)],
        compiler_params=params(LIMIT),
        cost_estimate=cost(7e9, 0),
        name="norm_query",
    )(tokens, norm_gain[None, :], q_weight, kv_weight, exponents)
    sums = with_others(sums, "gx")

    gate = pl.pallas_call(
        gate_kernel,
        out_shape=jax.ShapeDtypeStruct((rows, ff_dev), BF16),
        in_specs=[VMEM, VMEM],
        out_specs=VMEM,
        compiler_params=params(LIMIT),
        cost_estimate=cost(6e9, 16.8e6),
        name="gate",
    )(lhs, gate_weight)
    query, keyval, stats = pl.pallas_call(
        functools.partial(query_kernel, (gx, gy, seq_dev, q_dev, gx * width)),
        out_shape=(
            jax.ShapeDtypeStruct((rows, q_dev), BF16),
            jax.ShapeDtypeStruct((rows, 2 * head_dim), F32),
            jax.ShapeDtypeStruct((gx + 1, rows, 128), F32),
        ),
        in_specs=[VMEM] * gx,
        out_specs=(VMEM,) * 3,
        compiler_params=params(LIMIT),
        cost_estimate=cost(100000000, 100000),
        name="query_sum",
    )(*sums)
    queries = with_others(query, "gy")
    stay = packed_split(rows, each, ff_dev)
    both = pl.pallas_call(
        up_kernel,
        out_shape=jax.ShapeDtypeStruct((rows, ff_dev + stay + SPARE), BF16),
        in_specs=[VMEM] * 3 + [ANY],
        out_specs=VMEM,
        scratch_shapes=[pltpu.VMEM((rows, ff_dev + stay), F32)],
        compiler_params=params(LIMIT),
        cost_estimate=cost(6e9, 16.8e6),
        name="up",
    )(lhs, up_weight, gate, query)
    order = (1, 3, 2) if gx == 4 else tuple(range(1, gx))
    parts = with_others(both, "gx", order)

    position = jnp.pad(lengths.astype(F32)[:, None], ((0, 1), (0, 0)))
    angle = position * rotary_base**exponents
    tables = jnp.stack(
        [jnp.cos(angle), jnp.sin(angle), jnp.broadcast_to(position, angle.shape)]
    )
    *pieces, new_kv = pl.pallas_call(
        functools.partial(attention_kernel, (gy, gz, seq_dev)),
        out_shape=(jax.ShapeDtypeStruct((count, head_dim), BF16),) * gy
        + (jax.ShapeDtypeStruct((seq_dev, 2 * head_dim), BF16),),
        in_specs=[VMEM] * (gz + gy) + [VMEM, VMEM, ANY],
        out_specs=(VMEM,) * (gy + 1),
        scratch_shapes=[pltpu.VMEM((gy * count, head_dim), F32)] * 3,
        compiler_params=params(LIMIT),
        cost_estimate=cost(7e9, 2e6),
        name="attention",
    )(*queries, *caches, keyval, tables, both)
    pieces = pieces[:1] + [
        lax.ppermute(pieces[step], "gy", [(place, place ^ step) for place in range(gy)])
        for step in range(1, gy)
    ]
    pieces = with_others(jnp.stack(pieces), "gx")

    partial = pl.pallas_call(
        functools.partial(down_kernel, (gx, seq_dev, order)),
        out_shape=jax.ShapeDtypeStruct((rows, width), F32),
        in_specs=[VMEM] * (gx + 2),
        out_specs=VMEM,
        scratch_shapes=[
            pltpu.VMEM((rows, ff_dev), BF16),
            pltpu.VMEM((rows, max(ff_dev - stay, 128)), F32),
        ],
        compiler_params=params(LIMIT),
        cost_estimate=cost(4e9, 16.8e6),
        name="hidden_down",
    )(stats, *parts, down_weight)
    total, share = pl.pallas_call(
        functools.partial(out_kernel, (gx, gy, seq_dev)),
        out_shape=(
            jax.ShapeDtypeStruct((seqs, width), F32),
            jax.ShapeDtypeStruct((seqs, width), BF16),
        ),
        in_specs=[VMEM] * (gx + 2),
        out_specs=(VMEM, VMEM),
        scratch_shapes=[pltpu.VMEM((gy, each, q_dev), F32), pltpu.VMEM((rows, q_dev), F32)],
        compiler_params=params(LIMIT if gx <= FEW else 4 * LIMIT),
        cost_estimate=cost(1e9, 4e6),
        name="out_projection",
    )(*pieces, out_weight, partial)
    for other in with_others(share, ("gy", "gz"))[1:]:
        total = total + other.astype(F32)
    mixed = (tokens.astype(F32) + total).astype(BF16)
    return (mixed, new_kv)


def solution(mesh):
    in_specs = (
        P("group", "gx"),
        P("gx"),
        P("gx", ("gy", "gz")),
        P("gx", None),
        P(("gy", "gz"), "gx"),
        P("gx", ("gy", "gz")),
        P("gx", ("gy", "gz")),
        P(("gy", "gz"), "gx"),
        P(("group", "gy"), ("gx", "gz"), None),
        P(("group", "gy")),
    )
    out_specs = (P("group", "gx"), P(("group", "gy"), None))
    return jax.shard_map(body, mesh=mesh, in_specs=in_specs, out_specs=out_specs, check_vma=False)
```

```python
import functools

import jax
import jax.numpy as jnp
from jax import lax
from jax.experimental import pallas as pl
from jax.experimental.pallas import tpu as pltpu
from jax.sharding import PartitionSpec as P

epsilon = 1e-05
masked_fill = -1e30
rotary_base = 10000.0
FEW = 8
LIMIT = 3
SPARE = 512
F32 = jnp.float32
BF16 = jnp.bfloat16
VMEM = pl.BlockSpec(memory_space=pltpu.VMEM)
ANY = pl.BlockSpec(memory_space=pl.ANY)
HBM = pl.BlockSpec(memory_space=pltpu.HBM)
MIB = 2**20


def iota(shape, dim):
    return lax.broadcasted_iota(jnp.int32, shape, dim)


def thirds(values):
    high = values.astype(BF16).astype(F32)
    rest = values - high
    middle = rest.astype(BF16).astype(F32)
    return high, middle, rest - middle


def from_lanes(row, first, count):
    lane = iota(row.shape, 1)
    return jnp.sum(jnp.where((lane >= first) & (lane < first + count), row, 0.0), 1, keepdims=True)


def rotated_halves(values, cosine, sine):
    middle = values.shape[-1] // 2
    first, second = values[:, :middle], values[:, middle:]
    return jnp.concatenate(
        [first * cosine - second * sine, first * sine + second * cosine], 1
    )


def cost(flops, nbytes):
    return pl.CostEstimate(flops=int(flops), bytes_accessed=int(nbytes), transcendentals=0)


def params(mebibytes):
    return pltpu.CompilerParams(vmem_limit_bytes=mebibytes * MIB)


def exponent_kernel(table):
    table[...] = iota(table.shape, 1).astype(F32) / -table.shape[1]


def first_kernel(dims, tokens, gain, q_weight, kv_weight, after, sums, lhs, rows):
    gy, seq_dev = dims
    inputs = tokens[...].astype(F32)
    seqs, width = inputs.shape
    mean = jnp.sum(inputs, 1, keepdims=True) / width
    centred = inputs - mean
    square = jnp.sum(centred * centred, 1, keepdims=True)
    scaled = centred * gain[...]
    each = seq_dev + 1
    for a in range(gy):
        rows[a * each : a * each + seq_dev, :] = scaled[a * seq_dev : (a + 1) * seq_dev]
        rows[a * each + seq_dev : (a + 1) * each, :] = gain[...]
    lhs[...] = rows[...].astype(BF16)

    lanes = sums.shape[1] - q_weight.shape[1] - kv_weight.shape[1]
    lane = iota((seqs, lanes), 1)
    first = iota((seqs, lanes), 0) * 6
    marks = jnp.zeros((seqs, lanes), F32)
    for place, term in enumerate(thirds(mean) + thirds(square)):
        marks = jnp.where(lane == first + place, term, marks)
    marks = jnp.broadcast_to(jnp.sum(marks, 0, keepdims=True), (gy * each, lanes))

    values = lhs[...]
    query = jnp.dot(values, q_weight[...], preferred_element_type=F32)
    keyval = jnp.dot(values, kv_weight[...], preferred_element_type=F32)
    sums[...] = jnp.concatenate([query, keyval, marks], 1).astype(BF16)


def centring(dims, parts, width):
    gx, gy, seq_dev, features = dims
    each = seq_dev + 1
    place = iota((gy * each, 1), 0)
    valid = place % each < seq_dev
    first = (place // each * seq_dev + place % each) * 6
    means, squares = [], 0.0
    for part in parts:
        marks = part[:, width:].astype(F32)
        means.append(jnp.where(valid, from_lanes(marks, first, 3), 0.0))
        squares += from_lanes(marks, first + 3, 3)
    center = sum(means) / gx
    shifts = [mean - center for mean in means]
    spread = squares / features + sum(s * s for s in shifts) / gx
    return shifts, jnp.where(valid, lax.rsqrt(spread + epsilon), 0.0)


def shifted_sum(parts, shifts, seq_dev):
    total = 0.0
    for part, shift in zip(parts, shifts):
        part = part.astype(F32)
        total += part + shift * part[seq_dev : seq_dev + 1]
    return total


def product(lhs, weight, store, slab=1024):
    for start in range(0, weight.shape[1], slab):
        part = slice(start, min(start + slab, weight.shape[1]))
        store(part, jnp.dot(lhs, weight[:, part], preferred_element_type=F32))


def gate_kernel(lhs, weight, sums):
    def store(part, value):
        sums[:, part] = value.astype(BF16)

    product(lhs[...], weight, store)


def packed_split(rows, each, ff_dev):
    slab = ff_dev // rows * 2
    if rows == 2 * each and (rows - 1) * slab == 2 * ff_dev - slab and slab % 128 == 0:
        return ff_dev - slab
    return ff_dev


def up_kernel(lhs, weight, gate, after, both, wide):
    rows, ff_dev = gate.shape
    stay = wide.shape[1] - ff_dev
    wide[:, :ff_dev] = gate[...].astype(F32)

    def store(part, value):
        if part.start < stay:
            wide[:, ff_dev + part.start : ff_dev + part.stop] = value
        else:
            size = part.stop - part.start
            for r in range(rows - 1):
                wide[rows - 1 :, r * size : (r + 1) * size] = value[r : r + 1]

    product(lhs[...], weight, store, ff_dev - stay or 1024)
    both[:, : wide.shape[1]] = wide[...].astype(BF16)
    both[:, wide.shape[1] :] = jnp.zeros_like(both[:, wide.shape[1] :])


def query_kernel(dims, *refs):
    gx, gy, seq_dev, q_dev, features = dims
    parts, (query, keyval, stats) = refs[:gx], refs[gx:]
    width = q_dev + keyval.shape[1]
    shifts, inverse = centring((gx, gy, seq_dev, features), parts, width)
    for step in range(gx):
        stats[step] = jnp.broadcast_to(shifts[step], stats.shape[1:])
    stats[gx] = jnp.broadcast_to(inverse, stats.shape[1:])
    whole = shifted_sum([part[:, :width] for part in parts], shifts, seq_dev) * inverse
    query[...] = whole[:, :q_dev].astype(BF16)
    keyval[...] = whole[:, q_dev:]


def attention_kernel(dims, *refs):
    gy, gz, seq_dev = dims
    each = seq_dev + 1
    parts, refs = refs[:gy], refs[gy:]
    caches, refs = refs[:gz], refs[gz:]
    keyval, tables, after = refs[:3]
    pieces, (new_kv, qs, ks, vs) = refs[3 : 3 + gy], refs[3 + gy :]
    ctx_dev, head_dim = caches[0].shape[1], caches[0].shape[2] // 2
    heads_dev = parts[0].shape[1] // head_dim
    row = lax.axis_index("gy")

    def own_rows(values):
        mine = values[:each]
        for a in range(1, gy):
            mine = jnp.where(row == a, values[a * each : (a + 1) * each], mine)
        return mine

    cosine, sine, lengths = tables[0], tables[1], tables[2]
    fresh = own_rows(keyval[...])
    fresh = jnp.concatenate(
        [rotated_halves(fresh[:, :head_dim], cosine, sine), fresh[:, head_dim:]], 1
    ).astype(BF16)
    new_kv[...] = fresh[:seq_dev]
    fresh = fresh.astype(F32)
    for da in range(gy):
        query = own_rows(parts[da][...].astype(F32))
        for h in range(heads_dev):
            start = (da * heads_dev + h) * each
            part = slice(start, start + each)
            qs[part, :] = rotated_halves(query[:, h * head_dim : (h + 1) * head_dim], cosine, sine)
            ks[part, :] = fresh[:, :head_dim]
            vs[part, :] = fresh[:, head_dim:]

    count = heads_dev * each
    many = gy * count
    scale = head_dim ** (-0.5)
    queries = qs[...].astype(BF16)
    own = jnp.sum(queries.astype(F32) * ks[...], 1, keepdims=True) * scale
    sequence = iota((many, 1), 0) % each
    scores = []
    for db in range(gz):
        block = lax.axis_index("gx") * gz + (lax.axis_index("gz") ^ db)
        positions = (block * ctx_dev + iota((many, ctx_dev), 1)).astype(F32)
        found = jnp.full((many, ctx_dev), masked_fill, F32)
        for s in range(seq_dev):
            value = lax.dot_general(
                queries,
                caches[db][s, :, :head_dim],
                (((1,), (1,)), ((), ())),
                preferred_element_type=F32,
            )
            found = jnp.where((positions < lengths[s : s + 1, :1]) & (sequence == s), value * scale, found)
        scores.append(found)
    top = own
    for found in scores:
        top = jnp.maximum(top, jnp.max(found, 1, keepdims=True))
    own_weight = jnp.where(lax.axis_index("gx") == 0, jnp.exp(own - top), 0.0)
    denom = own_weight
    numer = own_weight * vs[...]
    for db in range(gz):
        weights = jnp.where(scores[db] > 0.5 * masked_fill, jnp.exp(scores[db] - top), 0.0)
        denom += jnp.sum(weights, 1, keepdims=True)
        for s in range(seq_dev):
            mine = jnp.where(sequence == s, weights, 0.0).astype(BF16)
            numer += jnp.dot(mine, caches[db][s, :, head_dim:], preferred_element_type=F32)

    lane = iota((many, head_dim), 1)
    terms = jnp.zeros((many, head_dim), F32)
    for j, term in enumerate(thirds(top) + thirds(denom)):
        terms = jnp.where((lane == sequence * 6 + j) & (sequence < seq_dev), term, terms)
    spare = jnp.zeros((many, head_dim), F32)
    for step in range(1, each):
        spare += pltpu.roll(terms, step, 0)
    out = jnp.where(sequence == seq_dev, spare, numer)
    for da in range(gy):
        pieces[da][...] = out[da * count : (da + 1) * count].astype(BF16)


def down_kernel(dims, stats, *refs):
    gx, seq_dev, order = dims
    parts, (down, result, hidden, left) = refs[:gx], refs[gx:]
    rows, ff_dev = hidden.shape
    stay = parts[0].shape[1] - ff_dev - SPARE
    slab = ff_dev - stay or min(ff_dev, 1024)
    inverse = stats[gx][:, :1]
    shifts = [stats[step][:, :1] for step in (0, *order)]

    def summed(start):
        found = [part[:, start : start + slab] for part in parts]
        return shifted_sum(found, shifts, seq_dev)

    if stay < ff_dev:
        left[...] = jnp.zeros_like(left)
        blocks = [
            [part[:, r * slab : (r + 1) * slab].astype(F32)[rows - 1 :] for r in range(rows - 1)]
            for part in parts
        ]
        for r in range(rows - 1):
            left[r : r + 1, :] = sum(
                block[r] + shift[r : r + 1] * block[seq_dev] for block, shift in zip(blocks, shifts)
            )
    for start in range(0, ff_dev, slab):
        gate = summed(start) * inverse
        upward = (summed(ff_dev + start) if start < stay else left[...]) * inverse
        hidden[:, start : start + slab] = (gate / (1.0 + jnp.exp(-gate)) * upward).astype(BF16)

    def store(part, value):
        result[:, part] = value

    product(hidden[...], down, store)


def out_kernel(dims, *refs):
    gx, gy, seq_dev = dims
    parts, (out_weight, partial, tokens, total, share, turned, att) = refs[:gx], refs[gx:]
    each = seq_dev + 1
    count, head_dim = parts[0].shape[1:]
    sequence = iota((count, 1), 0) % each
    valid = sequence < seq_dev
    lanes = min(128, head_dim)
    row = lax.axis_index("gy")
    for da in range(gy):
        values, tops, denoms = [], [], []
        for part in parts:
            piece = part[da].astype(F32)
            spare = jnp.where(valid, 0.0, piece[:, :lanes])
            marks = spare
            for step in range(1, each):
                marks += pltpu.roll(spare, count - step, 0)
            values.append(piece)
            tops.append(from_lanes(marks, sequence * 6, 3))
            denoms.append(from_lanes(marks, sequence * 6 + 3, 3))
        top = functools.reduce(jnp.maximum, tops)
        numer, denom = 0.0, 0.0
        for value, mine, part in zip(values, tops, denoms):
            factor = jnp.exp(mine - top)
            numer += value * factor
            denom += part * factor
        ratio = jnp.where(valid, numer / jnp.where(valid, denom, 1.0), 0.0)
        for h in range(count // each):
            turned[row ^ da, :, h * head_dim : (h + 1) * head_dim] = ratio[
                h * each : (h + 1) * each
            ]
    for a in range(gy):
        att[a * each : (a + 1) * each, :] = turned[a]
    result = partial[...] + jnp.dot(
        att[...].astype(BF16), out_weight[...], preferred_element_type=F32
    )
    for a in range(gy):
        total[a * seq_dev : (a + 1) * seq_dev, :] = result[a * each : a * each + seq_dev]
    share[...] = total[...].astype(BF16)
    total[...] += tokens[...].astype(F32)


def with_others(values, axis, order=None):
    size = lax.axis_size(axis)
    if size <= FEW:
        return [values] + [
            lax.ppermute(values, axis, [(place, place ^ step) for place in range(size)])
            for step in (order or range(1, size))
        ]
    gathered = lax.all_gather(values, axis)
    here = lax.axis_index(axis)
    return [
        lax.dynamic_index_in_dim(gathered, here ^ step, 0, False)
        for step in (0, *(order or range(1, size)))
    ]


def body(
    tokens,
    norm_gain,
    q_weight,
    kv_weight,
    out_weight,
    gate_weight,
    up_weight,
    down_weight,
    kv_cache,
    lengths,
):
    gx, gy, gz = (lax.axis_size(axis) for axis in ("gx", "gy", "gz"))
    seqs, width = tokens.shape
    seq_dev = lengths.shape[0]
    head_dim = kv_weight.shape[1] // 2
    q_dev = q_weight.shape[1]
    ff_dev = gate_weight.shape[1]
    each = seq_dev + 1
    rows = gy * each
    count = q_dev // head_dim * each
    lanes = -(-seqs * 6 // 128) * 128

    caches = with_others(kv_cache, "gz")

    exponents = pl.pallas_call(
        exponent_kernel,
        out_shape=jax.ShapeDtypeStruct((1, head_dim // 2), F32),
        out_specs=VMEM,
        compiler_params=params(LIMIT),
        cost_estimate=cost(7e9, 0),
        name="exponents",
    )()
    sums, lhs = pl.pallas_call(
        functools.partial(first_kernel, (gy, seq_dev)),
        out_shape=(
            jax.ShapeDtypeStruct((rows, q_dev + 2 * head_dim + lanes), BF16),
            jax.ShapeDtypeStruct((rows, width), BF16),
        ),
        in_specs=[VMEM] * 4 + [ANY],
        out_specs=(VMEM, VMEM),
        scratch_shapes=[pltpu.VMEM((rows, width), F32)],
        compiler_params=params(LIMIT),
        cost_estimate=cost(7e9, 0),
        name="norm_query",
    )(tokens, norm_gain[None, :], q_weight, kv_weight, exponents)
    sums = with_others(sums, "gx")

    gate = pl.pallas_call(
        gate_kernel,
        out_shape=jax.ShapeDtypeStruct((rows, ff_dev), BF16),
        in_specs=[VMEM, VMEM],
        out_specs=VMEM,
        compiler_params=params(LIMIT),
        cost_estimate=cost(6e9, 16.8e6),
        name="gate",
    )(lhs, gate_weight)
    query, keyval, stats = pl.pallas_call(
        functools.partial(query_kernel, (gx, gy, seq_dev, q_dev, gx * width)),
        out_shape=(
            jax.ShapeDtypeStruct((rows, q_dev), BF16),
            jax.ShapeDtypeStruct((rows, 2 * head_dim), F32),
            jax.ShapeDtypeStruct((gx + 1, rows, 128), F32),
        ),
        in_specs=[VMEM] * gx,
        out_specs=(VMEM,) * 3,
        compiler_params=params(LIMIT),
        cost_estimate=cost(100000000, 100000),
        name="query_sum",
    )(*sums)
    queries = with_others(query, "gy")
    stay = packed_split(rows, each, ff_dev)
    both = pl.pallas_call(
        up_kernel,
        out_shape=jax.ShapeDtypeStruct((rows, ff_dev + stay + SPARE), BF16),
        in_specs=[VMEM] * 3 + [ANY],
        out_specs=VMEM,
        scratch_shapes=[pltpu.VMEM((rows, ff_dev + stay), F32)],
        compiler_params=params(LIMIT),
        cost_estimate=cost(6e9, 16.8e6),
        name="up",
    )(lhs, up_weight, gate, query)
    order = (1, 3, 2) if gx == 4 else tuple(range(1, gx))
    parts = with_others(both, "gx", order)

    position = jnp.pad(lengths.astype(F32)[:, None], ((0, 1), (0, 0)))
    angle = position * rotary_base**exponents
    tables = jnp.stack(
        [jnp.cos(angle), jnp.sin(angle), jnp.broadcast_to(position, angle.shape)]
    )
    *pieces, new_kv = pl.pallas_call(
        functools.partial(attention_kernel, (gy, gz, seq_dev)),
        out_shape=(jax.ShapeDtypeStruct((count, head_dim), BF16),) * gy
        + (jax.ShapeDtypeStruct((seq_dev, 2 * head_dim), BF16),),
        in_specs=[VMEM] * (gz + gy) + [VMEM, VMEM, ANY],
        out_specs=(VMEM,) * (gy + 1),
        scratch_shapes=[pltpu.VMEM((gy * count, head_dim), F32)] * 3,
        compiler_params=params(LIMIT),
        cost_estimate=cost(7e9, 2e6),
        name="attention",
    )(*queries, *caches, keyval, tables, both)
    pieces = pieces[:1] + [
        lax.ppermute(pieces[step], "gy", [(place, place ^ step) for place in range(gy)])
        for step in range(1, gy)
    ]
    pieces = with_others(jnp.stack(pieces), "gx")

    partial = pl.pallas_call(
        functools.partial(down_kernel, (gx, seq_dev, order)),
        out_shape=jax.ShapeDtypeStruct((rows, width), F32),
        in_specs=[VMEM] * (gx + 2),
        out_specs=VMEM,
        scratch_shapes=[
            pltpu.VMEM((rows, ff_dev), BF16),
            pltpu.VMEM((rows, max(ff_dev - stay, 128)), F32),
        ],
        compiler_params=params(LIMIT),
        cost_estimate=cost(4e9, 16.8e6),
        name="hidden_down",
    )(stats, *parts, down_weight)
    total, share = pl.pallas_call(
        functools.partial(out_kernel, (gx, gy, seq_dev)),
        out_shape=(
            jax.ShapeDtypeStruct((seqs, width), F32),
            jax.ShapeDtypeStruct((seqs, width), BF16),
        ),
        in_specs=[VMEM] * (gx + 3),
        out_specs=(VMEM, VMEM),
        scratch_shapes=[pltpu.VMEM((gy, each, q_dev), F32), pltpu.VMEM((rows, q_dev), F32)],
        compiler_params=params(LIMIT if gx <= FEW else 4 * LIMIT),
        cost_estimate=cost(1e9, 4e6),
        name="out_projection",
    )(*pieces, out_weight, partial, tokens)
    for other in with_others(share, ("gy", "gz"))[1:]:
        total = total + other.astype(F32)
    return (total.astype(BF16), new_kv)


def solution(mesh):
    in_specs = (
        P("group", "gx"),
        P("gx"),
        P("gx", ("gy", "gz")),
        P("gx", None),
        P(("gy", "gz"), "gx"),
        P("gx", ("gy", "gz")),
        P("gx", ("gy", "gz")),
        P(("gy", "gz"), "gx"),
        P(("group", "gy"), ("gx", "gz"), None),
        P(("group", "gy")),
    )
    out_specs = (P("group", "gx"), P(("group", "gy"), None))
    return jax.shard_map(body, mesh=mesh, in_specs=in_specs, out_specs=out_specs, check_vma=False)
```
